128 devices in a mesh: wide: 32 (over y_hi, z, x), mp: 4 (over y_lo, core).
Axes of the slice: x: 4, y: 4 (y_hi: 2, y_lo: 2; y = y_hi * 2 + y_lo), z: 4, core: 2. Of those that a mesh axis runs over, the one named last changes fastest.
Arguments:
- context_kv: bfloat16 [2, 96, 1024, 512], P(None, 'wide', None, 'mp'), may hold values from -6 to 6
- train_order: int32 [96], replicated, may hold values from 0 to 95, each once
- prompt_lengths: int32 [96], replicated, may hold values from 128 to 1024, as said below
- parent_nodes: int32 [96, 128], P('wide'), may hold values from 0 to 127, as said below
- tree_mask: int32 [96, 128, 128], P('wide'), may hold values from 0 to 1, as said below
- tree_features: bfloat16 [96, 128, 8192], P('wide', None, 'mp'), may hold values from -7 to 7
- query_weight: bfloat16 [8192, 4096], P(None, 'mp'), may hold values from -0.0625 to 0.0625
- key_weight: bfloat16 [8192, 512], P(None, 'mp'), may hold values from -0.0625 to 0.0625
- value_weight: bfloat16 [8192, 512], P(None, 'mp'), may hold values from -0.0625 to 0.0625
- cotangent: bfloat16 [96, 128, 4096], P('wide', None, 'mp'), may hold values from -0.59765625 to 0.59765625
Outputs:
- attended: bfloat16 [96, 128, 4096], P('wide', None, 'mp')
- query_gradient: float32 [8192, 4096], P('wide', 'mp')
- key_gradient: float32 [8192, 512], P('wide', 'mp')
- value_gradient: float32 [8192, 512], P('wide', 'mp')
The draws below stay inside these ranges and needn't reach their ends.
Inputs may be any that keep to these rules, and one draw needn't show every extreme that they name: `train_order`: each prompt appears once. `prompt_lengths`: every prompt has at least 128 valid positions; some prompt has exactly 1024. `parent_nodes`: node i lies on level floor(i * 7 / 128); a node of level 0 is its own parent; any other node's parent is a node of the level just above it. tree_mask[r, i, j] is 1 exactly where node j is node i or one of its ancestors under parent_nodes[r], else 0.
All inputs are finite; a program needn't handle non-finite values.
Results may differ from the reference program's by a relative error of at most 0.03.
The reference program's roundings to bfloat16 on the way count: a program that leaves them out, or rounds other values in their place, can miss the bound.
Values may be sent and summed in bfloat16 or wider, within the bound.
A program may use at most 192 MiB of HBM per device.

```python
import jax
import jax.numpy as jnp
from jax import lax

D = 8192
QH = 32
KVH = 4
HEAD = 128
TREE = 128
LEVELS = 7
CTX = 1024
P_DEV = 3
PROMPTS = 96
N_WIDE = 32


def tree_parents(key):
    key = jax.random.fold_in(key, 11)
    node_ids = jnp.arange(TREE, dtype=jnp.int32)
    node_level = node_ids * LEVELS // TREE
    first_prev = ((node_level - 1) * TREE + LEVELS - 1) // LEVELS
    first_here = (node_level * TREE + LEVELS - 1) // LEVELS
    widths = jnp.maximum(first_here - first_prev, 1)
    raw_draw = jax.random.randint(key, (PROMPTS, TREE), 0, 1 << 20, dtype=jnp.int32)
    return jnp.where(node_level[None, :] == 0, node_ids[None, :], first_prev[None, :] + raw_draw % widths[None, :])


def draw_parent_nodes(key, part):
    return tree_parents(key)


def draw_tree_mask(key, part):
    parent_ids = tree_parents(key)
    identity = jnp.eye(TREE, dtype=jnp.int32)
    ancestry = jnp.broadcast_to(identity, (PROMPTS, TREE, TREE))
    for rounds in range(LEVELS):
        ancestry = jnp.maximum(identity[None, :, :], jnp.take_along_axis(ancestry, parent_ids[:, :, None], axis=1))
    return ancestry


def draw_prompt_lengths(key, part):
    key = jax.random.fold_in(key, 12)
    base_lengths = jax.random.randint(jax.random.fold_in(key, 1), (PROMPTS,), CTX // 8, CTX + 1, dtype=jnp.int32)
    longest = jax.random.randint(jax.random.fold_in(key, 2), (), 0, PROMPTS, dtype=jnp.int32)
    return jnp.where(jnp.arange(PROMPTS, dtype=jnp.int32) == longest, CTX, base_lengths).astype(jnp.int32)


def draw_tree_features(key, part):
    key = jax.random.fold_in(key, 13)
    values = jnp.clip(jax.random.normal(key, (PROMPTS, TREE, D), jnp.float32), -6.0, 6.0)
    return values.astype(jnp.bfloat16)


def block_scale(key, shape, pieces, low, top_value):
    loudness = 1.0
    for axis_at, shards_of in pieces:
        steps = jax.random.uniform(jax.random.fold_in(jax.random.fold_in(key, 6), axis_at), (shards_of,), jnp.float32, low / len(pieces), top_value / len(pieces))
        loudness = loudness * jnp.repeat(jnp.exp(steps), shape[axis_at] // shards_of).reshape((-1,) + (1,) * (len(shape) - 1 - axis_at))
    return loudness


def gaussian(own_key, extent, scale, most, split=(), kind=jnp.bfloat16):
    factor_of = block_scale(own_key, extent, split, -0.22, 0.18) if split else 1.0
    drawn = jax.random.normal(own_key, extent, jnp.float32) * scale * factor_of
    return jnp.minimum(jnp.maximum(drawn, -most), most).astype(kind)


def setup_inputs(seed: int = 0) -> dict:
    keys = jax.random.split(jax.random.key(seed), 11)
    context_kv = gaussian(keys[0], (2, PROMPTS, CTX, KVH * HEAD), 1.0, 6.0, ((1, 32), (3, 4)))
    train_order = jax.random.permutation(keys[1], PROMPTS).astype(jnp.int32)
    prompt_lengths = draw_prompt_lengths(jax.random.fold_in(keys[10], 71), 0)
    parent_nodes = draw_parent_nodes(jax.random.fold_in(keys[10], 71), 0)
    tree_mask = draw_tree_mask(jax.random.fold_in(keys[10], 71), 0)
    tree_features = draw_tree_features(jax.random.fold_in(keys[10], 71), 0)
    query_weight = gaussian(keys[6], (D, QH * HEAD), D ** -0.5, 0.0625, ((1, 4),))
    key_weight = gaussian(keys[7], (D, KVH * HEAD), D ** -0.5, 0.0625, ((1, 4),))
    value_weight = gaussian(keys[8], (D, KVH * HEAD), D ** -0.5, 0.0625, ((1, 4),))
    cotangent = gaussian(keys[9], (PROMPTS, TREE, QH * HEAD), 0.1, 0.59765625, ((0, 32), (2, 4)))
    return dict(context_kv=context_kv, train_order=train_order, prompt_lengths=prompt_lengths, parent_nodes=parent_nodes, tree_mask=tree_mask, tree_features=tree_features, query_weight=query_weight, key_weight=key_weight, value_weight=value_weight, cotangent=cotangent)


def attend_block(queries, tree_keys, tree_values, ctx_keys, ctx_values, lengths, masks, cotangent):
    scale = HEAD ** -0.5
    qfull = queries.astype(jnp.float32)
    tkfull = tree_keys.astype(jnp.float32)
    tvfull = tree_values.astype(jnp.float32)
    ckfull = ctx_keys.astype(jnp.float32)
    cvfull = ctx_values.astype(jnp.float32)
    positions = jnp.arange(ctx_keys.shape[1], dtype=jnp.int32)
    valid_ctx = (positions[None, :] < lengths[:, None])[:, None, None, None, :]
    valid_tree = (masks == 1)[:, None, None, :, :]
    score_ctx = jnp.einsum('pikgh,pckh->pkgic', qfull, ckfull) * scale
    score_tree = jnp.einsum('pikgh,pjkh->pkgij', qfull, tkfull) * scale
    score_ctx = jnp.where(valid_ctx, score_ctx, -1e30)
    score_tree = jnp.where(valid_tree, score_tree, -1e30)
    highest = jnp.maximum(jnp.max(score_ctx, axis=-1), jnp.max(score_tree, axis=-1))
    exp_ctx = jnp.where(valid_ctx, jnp.exp(score_ctx - highest[..., None]), 0.0)
    exp_tree = jnp.where(valid_tree, jnp.exp(score_tree - highest[..., None]), 0.0)
    totals = jnp.sum(exp_ctx, axis=-1) + jnp.sum(exp_tree, axis=-1)
    probs_ctx = exp_ctx / totals[..., None]
    probs_tree = exp_tree / totals[..., None]
    low_ctx = probs_ctx.astype(jnp.bfloat16).astype(jnp.float32)
    low_tree = probs_tree.astype(jnp.bfloat16).astype(jnp.float32)
    outputs = jnp.einsum('pkgic,pckh->pikgh', low_ctx, cvfull) + jnp.einsum('pkgij,pjkh->pikgh', low_tree, tvfull)
    attended = outputs.astype(jnp.bfloat16)
    dfull = cotangent.astype(jnp.float32)
    dprob_ctx = jnp.einsum('pikgh,pckh->pkgic', dfull, cvfull)
    dprob_tree = jnp.einsum('pikgh,pjkh->pkgij', dfull, tvfull)
    delta = jnp.sum(probs_ctx * dprob_ctx, axis=-1) + jnp.sum(probs_tree * dprob_tree, axis=-1)
    dscore_ctx = (probs_ctx * (dprob_ctx - delta[..., None]) * scale).astype(jnp.bfloat16).astype(jnp.float32)
    dscore_tree = (probs_tree * (dprob_tree - delta[..., None]) * scale).astype(jnp.bfloat16).astype(jnp.float32)
    dquery = (jnp.einsum('pkgic,pckh->pikgh', dscore_ctx, ckfull) + jnp.einsum('pkgij,pjkh->pikgh', dscore_tree, tkfull)).astype(jnp.bfloat16)
    dkey = jnp.einsum('pkgij,pikgh->pjkh', dscore_tree, qfull).astype(jnp.bfloat16)
    dvalue = jnp.einsum('pkgij,pikgh->pjkh', low_tree, dfull).astype(jnp.bfloat16)
    return attended, dquery, dkey, dvalue


def reference(context_kv, train_order, prompt_lengths, parent_nodes, tree_mask, tree_features, query_weight, key_weight, value_weight, cotangent):
    group = QH // KVH
    rows_block = P_DEV * TREE

    def block_step(running, block_id):
        first = (block_id * P_DEV).astype(jnp.int32)
        prompts = lax.dynamic_slice_in_dim(train_order, first, P_DEV, 0)
        features = lax.dynamic_slice_in_dim(tree_features, first, P_DEV, 0)
        parents = lax.dynamic_slice_in_dim(parent_nodes, first, P_DEV, 0)
        masks = lax.dynamic_slice_in_dim(tree_mask, first, P_DEV, 0)
        douts = lax.dynamic_slice_in_dim(cotangent, first, P_DEV, 0)
        lengths = jnp.take(prompt_lengths, prompts)
        context = jnp.take(context_kv, prompts, axis=1).reshape(2, P_DEV, CTX, KVH, HEAD)
        parent_feats = jnp.take_along_axis(features, parents[:, :, None], axis=1)
        node_inputs = (features.astype(jnp.float32) + parent_feats.astype(jnp.float32)).astype(jnp.bfloat16)
        flat = node_inputs.reshape(rows_block, D)
        queries = jnp.dot(flat, query_weight, preferred_element_type=jnp.float32).astype(jnp.bfloat16)
        tree_keys = jnp.dot(flat, key_weight, preferred_element_type=jnp.float32).astype(jnp.bfloat16)
        tree_values = jnp.dot(flat, value_weight, preferred_element_type=jnp.float32).astype(jnp.bfloat16)
        attended, dquery, dkey, dvalue = attend_block(
            queries.reshape(P_DEV, TREE, KVH, group, HEAD),
            tree_keys.reshape(P_DEV, TREE, KVH, HEAD),
            tree_values.reshape(P_DEV, TREE, KVH, HEAD),
            context[0], context[1], lengths, masks,
            douts.reshape(P_DEV, TREE, KVH, group, HEAD))
        grads_cat = jnp.concatenate([dquery.reshape(rows_block, QH * HEAD), dkey.reshape(rows_block, KVH * HEAD), dvalue.reshape(rows_block, KVH * HEAD)], axis=1)
        term = jnp.dot(flat.T, grads_cat, preferred_element_type=jnp.float32)
        rounded = lax.optimization_barrier(term.astype(jnp.bfloat16)).astype(jnp.float32)
        return running + rounded, attended.reshape(P_DEV, TREE, QH * HEAD)

    start_sum = jnp.zeros((D, (QH + 2 * KVH) * HEAD), jnp.float32)
    totals, blocks_out = lax.scan(block_step, start_sum, jnp.arange(N_WIDE, dtype=jnp.int32))
    attended = blocks_out.reshape(PROMPTS, TREE, QH * HEAD)
    query_gradient = totals[:, :QH * HEAD]
    key_gradient = totals[:, QH * HEAD:(QH + KVH) * HEAD]
    value_gradient = totals[:, (QH + KVH) * HEAD:]
    return attended, query_gradient, key_gradient, value_gradient
```

```python
import functools
import jax
import jax.numpy as jnp
from jax import lax
from jax.experimental import pallas as pl
from jax.experimental.pallas import tpu as pltpu
from jax.sharding import Mesh, PartitionSpec as P

HEAD = 128
TREE = 128
F32 = jnp.float32
BF16 = jnp.bfloat16


def _dot(a, b, dims):
    return lax.dot_general(a, b, (dims, ((), ())), preferred_element_type=F32)


def attend_kernel(chunk, len_ref, q_ref, tk_ref, tv_ref, ck_ref, cv_ref, mask_ref, cot_ref, out_ref, g_ref,
                  keys, values, bias):
    scale = HEAD ** (-0.5)
    ctx = ck_ref.shape[0]
    heads = q_ref.shape[1] // HEAD
    length = len_ref[pl.program_id(0)]
    keys[:ctx] = ck_ref[...]
    keys[ctx:] = tk_ref[...]
    values[:ctx] = cv_ref[...]
    values[ctx:] = tv_ref[...]
    cols = lax.broadcasted_iota(jnp.int32, (TREE, ctx), 1)
    bias[:, :ctx] = jnp.where(cols < length, 0.0, -1e30)
    bias[:, ctx:] = jnp.where(mask_ref[...] == 1, 0.0, -1e30)
    dkey = jnp.zeros((TREE, HEAD), F32)
    dvalue = jnp.zeros((TREE, HEAD), F32)
    for first in range(0, heads, chunk):
        def rows(ref):
            return jnp.concatenate([ref[:, h * HEAD:(h + 1) * HEAD] for h in range(first, first + chunk)], axis=0)
        q = rows(q_ref)
        cot = rows(cot_ref)
        s = _dot(q, keys[...], ((1,), (1,))) * scale
        s = (s.reshape(chunk, TREE, -1) + bias[...][None]).reshape(chunk * TREE, -1)
        e = jnp.exp(s - jnp.max(s, axis=1, keepdims=True))
        inv = 1.0 / jnp.sum(e, axis=1, keepdims=True)
        probs = e * inv
        low = probs.astype(BF16)
        dprob = _dot(cot, values[...], ((1,), (1,)))
        delta = jnp.sum(probs * dprob, axis=1, keepdims=True)
        dscore = ((probs * scale) * (dprob - delta)).astype(BF16)
        out = _dot(low, values[...], ((1,), (0,))).astype(BF16)
        dq = _dot(dscore, keys[...], ((1,), (0,))).astype(BF16)
        for k in range(chunk):
            h = first + k
            out_ref[:, h * HEAD:(h + 1) * HEAD] = out[k * TREE:(k + 1) * TREE]
            g_ref[:, h * HEAD:(h + 1) * HEAD] = dq[k * TREE:(k + 1) * TREE]
        dkey += _dot(dscore[:, ctx:], q, ((0,), (0,)))
        dvalue += _dot(low[:, ctx:], cot, ((0,), (0,)))
    g_ref[:, heads * HEAD:(heads + 1) * HEAD] = dkey.astype(BF16)
    g_ref[:, (heads + 1) * HEAD:] = dvalue.astype(BF16)


def attend(lengths, queries, tree_keys, tree_values, ctx_keys, ctx_values, masks, cotangent, chunk=2):
    rows, q_cols = queries.shape
    slots = rows // TREE
    ctx = ctx_keys.shape[1]
    row = lambda cols: pl.BlockSpec((TREE, cols), lambda s: (s, 0))
    per = lambda n, cols: pl.BlockSpec((None, n, cols), lambda s: (s, 0, 0))
    return pl.pallas_call(
        functools.partial(attend_kernel, chunk),
        grid=(slots,),
        in_specs=[pl.BlockSpec(memory_space=pltpu.SMEM), row(q_cols), row(HEAD), row(HEAD),
                  per(ctx, HEAD), per(ctx, HEAD), per(TREE, TREE), row(q_cols)],
        out_specs=[row(q_cols), row(q_cols + 2 * HEAD)],
        out_shape=[jax.ShapeDtypeStruct((rows, q_cols), BF16), jax.ShapeDtypeStruct((rows, q_cols + 2 * HEAD), BF16)],
        scratch_shapes=[pltpu.VMEM((ctx + TREE, HEAD), BF16), pltpu.VMEM((ctx + TREE, HEAD), BF16),
                        pltpu.VMEM((TREE, ctx + TREE), F32)],
        compiler_params=pltpu.CompilerParams(vmem_limit_bytes=48 * 1024 * 1024),
    )(lengths, queries, tree_keys, tree_values, ctx_keys, ctx_values, masks, cotangent)


WIDE = ("y_hi", "z", "x")
MP = ("y_lo", "core")


def local(
    context_kv,
    train_order,
    prompt_lengths,
    parent_nodes,
    tree_mask,
    tree_features,
    query_weight,
    key_weight,
    value_weight,
    cotangent,
):
    slots_dev = tree_features.shape[0]
    rows_dev = slots_dev * TREE
    n_x = lax.axis_size("x")
    n_yz = lax.axis_size("y_hi") * lax.axis_size("z")
    my_index = lax.axis_index(WIDE)
    spread_kv = lax.all_to_all(context_kv, WIDE, split_axis=2, concat_axis=1, tiled=True)
    permuted = jnp.take(spread_kv, train_order, axis=1)
    context = lax.all_to_all(permuted, WIDE, split_axis=1, concat_axis=2, tiled=True)
    my_prompts = lax.dynamic_slice_in_dim(train_order, my_index * slots_dev, slots_dev, 0)
    lengths = jnp.take(prompt_lengths, my_prompts)
    nodes = jnp.arange(TREE, dtype=jnp.int32)
    pick = (parent_nodes[:, :, None] == nodes).astype(BF16) + jnp.eye(TREE, dtype=BF16)
    input_shard = jnp.einsum("pij,pjd->pid", pick, tree_features, preferred_element_type=F32).astype(BF16)
    node_inputs = lax.all_gather(input_shard, MP, axis=2, tiled=True)
    flat = node_inputs.reshape(rows_dev, node_inputs.shape[2])
    queries = jnp.dot(flat, query_weight, preferred_element_type=F32).astype(BF16)
    tree_keys = jnp.dot(flat, key_weight, preferred_element_type=F32).astype(BF16)
    tree_values = jnp.dot(flat, value_weight, preferred_element_type=F32).astype(BF16)
    q_cols = query_weight.shape[1]
    kv_cols = key_weight.shape[1]
    attended, grads = attend(
        lengths, queries, tree_keys, tree_values, context[0], context[1], tree_mask,
        cotangent.reshape(rows_dev, q_cols),
    )
    parts = flat.reshape(rows_dev, n_yz, n_x, -1)
    group_flat = lax.all_to_all(parts, "x", split_axis=2, concat_axis=0, tiled=True)
    group_flat = group_flat.reshape(rows_dev * n_x, -1)
    group_grads = lax.all_gather(grads, "x", axis=0, tiled=True)
    term = jnp.einsum("rd,rc->dc", group_flat, group_grads, preferred_element_type=F32).astype(BF16)
    summed = lax.psum_scatter(term, ("y_hi", "z"), scatter_dimension=0, tiled=True).astype(F32)
    query_gradient = summed[:, :q_cols]
    key_gradient = summed[:, q_cols : q_cols + kv_cols]
    value_gradient = summed[:, q_cols + kv_cols :]
    return (attended.reshape(slots_dev, TREE, q_cols), query_gradient, key_gradient, value_gradient)


def solution(mesh):
    cube = Mesh(mesh.devices.reshape(2, 4, 4, 2, 2), WIDE + MP)
    return jax.shard_map(
        local,
        mesh=cube,
        in_specs=(
            P(None, WIDE, None, MP),
            P(),
            P(),
            P(WIDE, None),
            P(WIDE, None, None),
            P(WIDE, None, MP),
            P(None, MP),
            P(None, MP),
            P(None, MP),
            P(WIDE, None, MP),
        ),
        out_specs=(P(WIDE, None, MP), P(WIDE, MP), P(WIDE, MP), P(WIDE, MP)),
        check_vma=False,
    )
```

```python
import functools

import jax
import jax.numpy as jnp
from jax import lax
from jax.experimental import pallas as pl
from jax.experimental.pallas import tpu as pltpu
from jax.sharding import Mesh, PartitionSpec as P

HEAD = 128
TREE = 128
F32 = jnp.float32
BF16 = jnp.bfloat16
MESH = pl.DeviceIdType.MESH
WIDE = ("y_hi", "z", "x")
MP = ("y_lo", "core")


def _dot(a, b, dims):
    return lax.dot_general(a, b, (dims, ((), ())), preferred_element_type=F32)


def _peer(axis, step):
    return {axis: lax.rem(lax.axis_index(axis) + step, lax.axis_size(axis))}


def _at(offset, size):
    return pl.ds(pl.multiple_of(offset, size), size)


def attend_slot(chunk, s, length, q_ref, tk_ref, tv_ref, ck_ref, cv_ref, mask_ref, cot_ref, out_ref,
                keys, values, bias, put_grad):
    scale = HEAD ** (-0.5)
    ctx = ck_ref.shape[1]
    heads = q_ref.shape[1] // HEAD
    here = _at(s * TREE, TREE)
    keys[:ctx] = ck_ref[s]
    keys[ctx:] = tk_ref[here, :]
    values[:ctx] = cv_ref[s]
    values[ctx:] = tv_ref[here, :]
    cols = lax.broadcasted_iota(jnp.int32, (TREE, ctx), 1)
    bias[:, :ctx] = jnp.where(cols < length, 0.0, -1e30)
    bias[:, ctx:] = jnp.where(mask_ref[s] == 1, 0.0, -1e30)
    dkey = jnp.zeros((HEAD, TREE), F32)
    dvalue = jnp.zeros((HEAD, TREE), F32)
    for first in range(0, heads, chunk):
        def rows(ref):
            return jnp.concatenate(
                [ref[here, h * HEAD:(h + 1) * HEAD] for h in range(first, first + chunk)], axis=0)
        q = rows(q_ref)
        cot = rows(cot_ref)
        score = _dot(q, keys[...], ((1,), (1,))) * scale
        score = (score.reshape(chunk, TREE, -1) + bias[...][None]).reshape(chunk * TREE, -1)
        e = jnp.exp(score - jnp.max(score, axis=1, keepdims=True))
        probs = e * (1.0 / jnp.sum(e, axis=1, keepdims=True))
        low = probs.astype(BF16)
        dprob = _dot(cot, values[...], ((1,), (1,)))
        delta = jnp.sum(probs * dprob, axis=1, keepdims=True)
        dscore = ((probs * scale) * (dprob - delta)).astype(BF16)
        out = _dot(low, values[...], ((1,), (0,))).astype(BF16)
        dq = _dot(dscore, keys[...], ((1,), (0,)))
        for k in range(chunk):
            h = first + k
            out_ref[here, h * HEAD:(h + 1) * HEAD] = out[k * TREE:(k + 1) * TREE]
            put_grad(h, dq[k * TREE:(k + 1) * TREE].T.astype(BF16))
        dkey += _dot(q, dscore[:, ctx:], ((0,), (0,)))
        dvalue += _dot(cot, low[:, ctx:], ((0,), (0,)))
    put_grad(heads, dkey.astype(BF16))
    put_grad(heads + 1, dvalue.astype(BF16))


def late_kernel(len_ref, q_ref, tk_ref, tv_ref, ck_ref, cv_ref, mask_ref, cot_ref, flat_ref,
                out_ref, grad_ref,
                keys, values, bias, group_flat, group_grad, term, arrived, own, across, landed,
                flat_send, flat_recv, pass_send, pass_recv, grad_send, grad_recv, term_send, term_recv,
                y_send, y_recv, copy_sem):
    axes = ("x", "z")
    n = lax.axis_size("x")
    rows = q_ref.shape[0]
    slots = rows // TREE
    half_cols = group_grad.shape[1]
    blocks = half_cols // HEAD
    core = lax.axis_index("core")
    here = [lax.axis_index(a) for a in axes]
    y_me = lax.axis_index("y_hi")

    barrier = pltpu.get_barrier_semaphore()
    partners = [_peer(a, d) for a in axes for d in range(1, n)] + [_peer("core", 1), _peer("y_hi", 1)]
    for p in partners:
        pl.semaphore_signal(barrier, inc=1, device_id=p, device_id_type=MESH)
    pl.semaphore_wait(barrier, len(partners))

    def piece(half, at):
        return flat_ref.at[core, :, at] if half == 0 else flat_ref.at[core, at]

    def flat_copy(half, d):
        to = _peer(axes[half], d)
        return pltpu.make_async_remote_copy(
            src_ref=piece(half, to[axes[half]]),
            dst_ref=group_flat.at[half, core, :, _at(here[half] * rows, rows)],
            send_sem=flat_send.at[half, d - 1], recv_sem=flat_recv.at[half, d - 1],
            device_id=to, device_id_type=MESH)

    def pass_copy(half, d):
        member = lax.rem(here[half] + n - d, n)
        ref = group_flat.at[half, core, :, _at(member * rows, rows)]
        return pltpu.make_async_remote_copy(
            src_ref=ref, dst_ref=ref, send_sem=pass_send.at[half, d - 1], recv_sem=pass_recv.at[half, d - 1],
            device_id=_peer("core", 1), device_id_type=MESH)

    def own_copy(half, y):
        src = flat_ref.at[y, :, here[half]] if half == 0 else flat_ref.at[y, here[half]]
        return pltpu.make_async_copy(src, group_flat.at[half, y, :, _at(here[half] * rows, rows)], copy_sem.at[half, y])

    def grad_copy(half, s, d):
        ref = group_grad.at[half, :, _at((here[half] * slots + s) * TREE, TREE)]
        return pltpu.make_async_remote_copy(
            src_ref=ref, dst_ref=ref, send_sem=grad_send.at[half, s, d - 1], recv_sem=grad_recv.at[half, s, d - 1],
            device_id=_peer(axes[half], d), device_id_type=MESH)

    def term_copy(half, d):
        return pltpu.make_async_remote_copy(
            src_ref=term.at[half, d - 1], dst_ref=arrived.at[half, d - 1],
            send_sem=term_send.at[half, d - 1], recv_sem=term_recv.at[half, d - 1],
            device_id=_peer(axes[1 - half], d), device_id_type=MESH)

    def y_copy(half):
        return pltpu.make_async_remote_copy(
            src_ref=across.at[half], dst_ref=landed.at[half], send_sem=y_send.at[half], recv_sem=y_recv.at[half],
            device_id=_peer("y_hi", 1), device_id_type=MESH)

    both = [(half, d) for d in range(1, n) for half in range(2)]
    for half, d in both:
        flat_copy(half, d).start()
    for half in range(2):
        for y in range(2):
            own_copy(half, y).start()

    def slot_step(s, carry):
        def put_grad(column, block):
            half, at = divmod(column, blocks)
            group_grad[half, at * HEAD:(at + 1) * HEAD, _at((here[half] * slots + s) * TREE, TREE)] = block
        attend_slot(2, s, len_ref[s], q_ref, tk_ref, tv_ref, ck_ref, cv_ref, mask_ref, cot_ref, out_ref,
                    keys, values, bias, put_grad)
        for half, d in both:
            grad_copy(half, s, d).start()
        return carry

    lax.fori_loop(0, slots, slot_step, 0)

    for half, d in both:
        flat_copy(half, d).wait_recv()
        pass_copy(half, d).start()
    for half in range(2):
        for y in range(2):
            own_copy(half, y).wait()
    for half, d in both:
        pass_copy(half, d).wait_recv()
    for s in range(slots):
        for half, d in both:
            grad_copy(half, s, d).wait_recv()

    def product(half, d, y):
        at = lax.rem(here[1 - half] + d, n)
        return _dot(group_grad[half], group_flat[half, y, at], ((1,), (0,)))

    for half, d in both:
        def block_step(y, carry, half=half, d=d):
            term[half, d - 1, y] = product(half, d, y).astype(BF16)
            return carry
        lax.fori_loop(0, 2, block_step, 0)
        term_copy(half, d).start()
    for half in range(2):
        def own_step(y, carry, half=half):
            own[half, y] = product(half, 0, y)
            return carry
        lax.fori_loop(0, 2, own_step, 0)
    for half, d in both:
        term_copy(half, d).wait_recv()

    def total(half, y):
        out = own[half, y]
        for d in range(1, n):
            out += arrived[half, d - 1, y].astype(F32)
        return out

    for half in range(2):
        across[half] = total(half, 1 - y_me).astype(BF16)
        y_copy(half).start()
    for half in range(2):
        own[half, y_me] = total(half, y_me)
    for half in range(2):
        y_copy(half).wait_recv()
        grad_ref[:, half * half_cols:(half + 1) * half_cols] = (own[half, y_me] + landed[half].astype(F32)).T

    for half, d in both:
        flat_copy(half, d).wait_send()
        pass_copy(half, d).wait_send()
        term_copy(half, d).wait_send()
        for s in range(slots):
            grad_copy(half, s, d).wait_send()
    for half in range(2):
        y_copy(half).wait_send()


def late(lengths, queries, tree_keys, tree_values, ctx_keys, ctx_values, masks, cotangent, flat):
    rows, q_cols = queries.shape
    slots = rows // TREE
    ctx = ctx_keys.shape[1]
    cols = q_cols + 2 * HEAD
    n_y, n, _, _, width = flat.shape
    half_cols = cols // 2
    vmem = pl.BlockSpec(memory_space=pltpu.VMEM)
    dma = pltpu.SemaphoreType.DMA
    return pl.pallas_call(
        late_kernel,
        in_specs=[pl.BlockSpec(memory_space=pltpu.SMEM)] + [vmem] * 8,
        out_specs=[vmem, vmem],
        out_shape=[jax.ShapeDtypeStruct((rows, q_cols), BF16), jax.ShapeDtypeStruct((width, cols), F32)],
        scratch_shapes=[
            pltpu.VMEM((ctx + TREE, HEAD), BF16),
            pltpu.VMEM((ctx + TREE, HEAD), BF16),
            pltpu.VMEM((TREE, ctx + TREE), F32),
            pltpu.VMEM((2, n_y, n, n * rows, width), BF16),
            pltpu.VMEM((2, half_cols, n * rows), BF16),
            pltpu.VMEM((2, n - 1, n_y, half_cols, width), BF16),
            pltpu.VMEM((2, n - 1, n_y, half_cols, width), BF16),
            pltpu.VMEM((2, n_y, half_cols, width), F32),
            pltpu.VMEM((2, half_cols, width), BF16),
            pltpu.VMEM((2, half_cols, width), BF16),
            dma((2, n - 1)), dma((2, n - 1)), dma((2, n - 1)), dma((2, n - 1)),
            dma((2, slots, n - 1)), dma((2, slots, n - 1)), dma((2, n - 1)), dma((2, n - 1)),
            dma((2,)), dma((2,)), dma((2, 2)),
        ],
        compiler_params=pltpu.CompilerParams(
            collective_id=0, has_side_effects=True, vmem_limit_bytes=60 * 1024 * 1024),
    )(lengths, queries, tree_keys, tree_values, ctx_keys, ctx_values, masks, cotangent, flat)


def local(
    context_kv,
    train_order,
    prompt_lengths,
    parent_nodes,
    tree_mask,
    tree_features,
    query_weight,
    key_weight,
    value_weight,
    cotangent,
):
    slots_dev = tree_features.shape[0]
    rows_dev = slots_dev * TREE
    sizes = [lax.axis_size(a) for a in WIDE]
    my_index = lax.axis_index(WIDE)
    spread_kv = lax.all_to_all(context_kv, WIDE, split_axis=2, concat_axis=1, tiled=True)
    permuted = jnp.take(spread_kv, train_order, axis=1)
    context = lax.all_to_all(permuted, WIDE, split_axis=1, concat_axis=2, tiled=True)
    my_prompts = lax.dynamic_slice_in_dim(train_order, my_index * slots_dev, slots_dev, 0)
    lengths = jnp.take(prompt_lengths, my_prompts)
    nodes = jnp.arange(TREE, dtype=jnp.int32)
    pick = (parent_nodes[:, :, None] == nodes).astype(BF16) + jnp.eye(TREE, dtype=BF16)
    input_shard = jnp.einsum("pij,pjd->pid", pick, tree_features, preferred_element_type=F32).astype(BF16)
    node_inputs = lax.all_gather(input_shard, MP, axis=2, tiled=True)
    flat = node_inputs.reshape(rows_dev, node_inputs.shape[2])
    queries = jnp.dot(flat, query_weight, preferred_element_type=F32).astype(BF16)
    tree_keys = jnp.dot(flat, key_weight, preferred_element_type=F32).astype(BF16)
    tree_values = jnp.dot(flat, value_weight, preferred_element_type=F32).astype(BF16)
    q_cols = query_weight.shape[1]
    kv_cols = key_weight.shape[1]
    blocks = flat.reshape(rows_dev, *sizes, -1).transpose(1, 2, 3, 0, 4)
    attended, summed = late(
        lengths, queries, tree_keys, tree_values, context[0], context[1], tree_mask,
        cotangent.reshape(rows_dev, q_cols), blocks,
    )
    query_gradient = summed[:, :q_cols]
    key_gradient = summed[:, q_cols : q_cols + kv_cols]
    value_gradient = summed[:, q_cols + kv_cols :]
    return (attended.reshape(slots_dev, TREE, q_cols), query_gradient, key_gradient, value_gradient)


def solution(mesh):
    cube = Mesh(mesh.devices.reshape(2, 4, 4, 2, 2), WIDE + MP)
    return jax.shard_map(
        local,
        mesh=cube,
        in_specs=(
            P(None, WIDE, None, MP),
            P(),
            P(),
            P(WIDE, None),
            P(WIDE, None, None),
            P(WIDE, None, MP),
            P(None, MP),
            P(None, MP),
            P(None, MP),
            P(WIDE, None, MP),
        ),
        out_specs=(P(WIDE, None, MP), P(WIDE, MP), P(WIDE, MP), P(WIDE, MP)),
        check_vma=False,
    )
```

```python
import functools

import jax
import jax.numpy as jnp
from jax import lax
from jax.experimental import pallas as pl
from jax.experimental.pallas import tpu as pltpu
from jax.sharding import Mesh, PartitionSpec as P

HEAD = 128
TREE = 128
F32 = jnp.float32
BF16 = jnp.bfloat16
MESH = pl.DeviceIdType.MESH
WIDE = ("y_hi", "z", "x")
MP = ("y_lo", "core")


def _dot(a, b, dims):
    return lax.dot_general(a, b, (dims, ((), ())), preferred_element_type=F32)


def _peer(axis, step):
    return {axis: lax.rem(lax.axis_index(axis) + step, lax.axis_size(axis))}


def _at(offset, size):
    return pl.ds(pl.multiple_of(offset, size), size)


def attend_slot(chunk, s, length, qkv, kv, mask_ref, cot_ref, out_ref, bias, put_grad):
    scale = HEAD ** (-0.5)
    ctx = kv.shape[2] - TREE
    heads = cot_ref.shape[1] // HEAD
    here = _at(s * TREE, TREE)
    cols = lax.broadcasted_iota(jnp.int32, (TREE, ctx), 1)
    bias[:, :ctx] = jnp.where(cols < length, 0.0, -1e30)
    bias[:, ctx:] = jnp.where(mask_ref[s] == 1, 0.0, -1e30)
    dkey = jnp.zeros((HEAD, TREE), F32)
    dvalue = jnp.zeros((HEAD, TREE), F32)
    for first in range(0, heads, chunk):
        def rows(ref):
            return jnp.concatenate(
                [ref[here, h * HEAD:(h + 1) * HEAD] for h in range(first, first + chunk)], axis=0)
        q = rows(qkv)
        cot = rows(cot_ref)
        score = _dot(q, kv[0, s], ((1,), (1,))) * scale
        score = (score.reshape(chunk, TREE, -1) + bias[...][None]).reshape(chunk * TREE, -1)
        e = jnp.exp(score - jnp.max(score, axis=1, keepdims=True))
        probs = e * (1.0 / jnp.sum(e, axis=1, keepdims=True))
        low = probs.astype(BF16)
        dprob = _dot(cot, kv[1, s], ((1,), (1,)))
        delta = jnp.sum(probs * dprob, axis=1, keepdims=True)
        dscore = ((probs * scale) * (dprob - delta)).astype(BF16)
        out = _dot(low, kv[1, s], ((1,), (0,))).astype(BF16)
        dq = _dot(dscore, kv[0, s], ((1,), (0,)))
        for k in range(chunk):
            h = first + k
            out_ref[here, h * HEAD:(h + 1) * HEAD] = out[k * TREE:(k + 1) * TREE]
            put_grad(h, dq[k * TREE:(k + 1) * TREE].T.astype(BF16))
        dkey += _dot(q, dscore[:, ctx:], ((0,), (0,)))
        dvalue += _dot(cot, low[:, ctx:], ((0,), (0,)))
    put_grad(heads, dkey.astype(BF16))
    put_grad(heads + 1, dvalue.astype(BF16))


def train_kernel(order_ref, len_ref, parent_ref, feat_ref, mask_ref, cot_ref, ctx_ref, wq_ref, wk_ref, wv_ref,
                 out_ref, gq_ref, gk_ref, gv_ref,
                 spread, staged, kv, flat, weight, acc, qkv, bias,
                 group_flat, group_grad, term, arrived, own, across, landed,
                 ctx_send, ctx_recv, slot_send, slot_recv, mp_send, mp_recv, weight_sem,
                 flat_send, flat_recv, pass_send, pass_recv, grad_send, grad_recv, term_send, term_recv,
                 y_send, y_recv, copy_sem):
    axes = ("x", "z")
    n = lax.axis_size("x")
    n_y = lax.axis_size("y_hi")
    wide = n_y * n * n
    slots = mask_ref.shape[0]
    rows = slots * TREE
    width = flat.shape[4]
    part = spread.shape[2]
    half_cols = group_grad.shape[1]
    blocks = half_cols // HEAD
    core = lax.axis_index("core")
    y_lo = lax.axis_index("y_lo")
    here = [lax.axis_index(a) for a in axes]
    y_me = lax.axis_index("y_hi")
    me = (y_me * n + here[1]) * n + here[0]

    def trainer(index):
        return {"y_hi": index // (n * n), "z": lax.rem(index // n, n), "x": lax.rem(index, n)}

    barrier = pltpu.get_barrier_semaphore()

    def greet(d, carry):
        pl.semaphore_signal(barrier, inc=1, device_id=trainer(lax.rem(me + d, wide)), device_id_type=MESH)
        return carry

    lax.fori_loop(1, wide, greet, 0)
    for axis in MP:
        pl.semaphore_signal(barrier, inc=1, device_id=_peer(axis, 1), device_id_type=MESH)
    pl.semaphore_wait(barrier, wide + 1)

    def spread_copy(d):
        to = lax.rem(me + d, wide)
        return pltpu.make_async_remote_copy(
            src_ref=ctx_ref.at[:, :, _at(to * part, part)], dst_ref=spread.at[:, pl.ds(me * slots, slots)],
            send_sem=ctx_send.at[d], recv_sem=ctx_recv.at[d], device_id=trainer(to), device_id_type=MESH)

    def slot_copy(s, d):
        to = lax.rem(me + d, wide)
        return pltpu.make_async_remote_copy(
            src_ref=staged.at[:, to * slots + s], dst_ref=kv.at[:, s, _at(me * part, part)],
            send_sem=slot_send.at[s, d], recv_sem=slot_recv.at[s, d], device_id=trainer(to), device_id_type=MESH)

    def start(copy):
        def step(d, carry):
            copy(d).start()
            return carry
        lax.fori_loop(1, wide, step, 0)

    def finish(copy):
        def step(d, carry):
            copy(d).wait_recv()
            return carry
        lax.fori_loop(1, wide, step, 0)

    def finish_send(copy):
        def step(d, carry):
            copy(d).wait_send()
            return carry
        lax.fori_loop(1, wide, step, 0)

    own_ctx = pltpu.make_async_copy(
        ctx_ref.at[:, :, _at(me * part, part)], spread.at[:, pl.ds(me * slots, slots)], ctx_recv.at[0])
    start(spread_copy)
    own_ctx.start()

    def shard(a, c):
        return flat.at[a, pl.ds(c * 2, 2)]

    def mp_copy(k):
        a = (y_lo, y_lo, 1 - y_lo)[k]
        return pltpu.make_async_remote_copy(
            src_ref=shard(a, core), dst_ref=shard(a, core), send_sem=mp_send.at[k], recv_sem=mp_recv.at[k],
            device_id=_peer("y_lo" if k == 0 else "core", 1), device_id_type=MESH)

    depth = weight.shape[1]
    buffers = weight.shape[0]
    sources = [(y_lo, core), (y_lo, 1 - core), (1 - y_lo, core), (1 - y_lo, 1 - core)]
    chunks = [(a, 2 * c + k) for a, c in sources for k in range(2)]

    def weight_copies(i):
        a, z = chunks[i]
        at = _at((a * n + z) * depth, depth)
        slot = i % buffers
        q_cols, kv_cols = wq_ref.shape[1], wk_ref.shape[1]
        return [
            pltpu.make_async_copy(wq_ref.at[at], weight.at[slot, :, :q_cols], weight_sem.at[slot, 0]),
            pltpu.make_async_copy(wk_ref.at[at], weight.at[slot, :, q_cols:q_cols + kv_cols], weight_sem.at[slot, 1]),
            pltpu.make_async_copy(wv_ref.at[at], weight.at[slot, :, q_cols + kv_cols:], weight_sem.at[slot, 2]),
        ]

    for i in range(buffers):
        for c in weight_copies(i):
            c.start()

    for s in range(slots):
        node = lax.broadcasted_iota(jnp.int32, (TREE, TREE), 0)
        same = node == lax.broadcasted_iota(jnp.int32, (TREE, TREE), 1)
        pick = (node == parent_ref[s:s + 1, :]).astype(F32) + same.astype(F32)
        mixed = _dot(pick.astype(BF16), feat_ref[s], ((0,), (0,))).astype(BF16)
        for k in range(2):
            for x in range(n):
                at = (k * n + x) * width
                flat[y_lo, 2 * core + k, x, s * TREE:(s + 1) * TREE, :] = mixed[:, at:at + width]
    mp_copy(0).start()
    mp_copy(1).start()

    def project(i):
        a, z = chunks[i]
        for c in weight_copies(i):
            c.wait()
        lhs = jnp.concatenate([flat[a, z, x] for x in range(n)], axis=1)
        product = _dot(lhs, weight[i % buffers], ((1,), (0,)))
        if i == 0:
            acc[...] = product
        else:
            acc[...] += product
        if i + buffers < len(chunks):
            for c in weight_copies(i + buffers):
                c.start()

    project(0)
    project(1)
    mp_copy(1).wait_recv()
    project(2)
    project(3)

    finish(spread_copy)
    own_ctx.wait()

    def place(r, carry):
        staged[:, r] = spread[:, order_ref[r]]
        return carry

    lax.fori_loop(0, wide * slots, place, 0)
    for s in range(slots):
        start(functools.partial(slot_copy, s))
    own_slots = pltpu.make_async_copy(
        staged.at[:, pl.ds(me * slots, slots)], kv.at[:, :, _at(me * part, part)], slot_recv.at[0, 0])
    own_slots.start()

    def flat_copy(half, d):
        to = _peer(axes[half], d)
        at = to[axes[half]]
        mine = pl.ds(core * 2, 2)
        dst = _at(here[half] * rows, rows)
        return pltpu.make_async_remote_copy(
            src_ref=flat.at[:, mine, at] if half == 0 else flat.at[:, at, mine],
            dst_ref=group_flat.at[half, :, mine, dst],
            send_sem=flat_send.at[half, d - 1], recv_sem=flat_recv.at[half, d - 1],
            device_id=to, device_id_type=MESH)

    def pass_copy(half, d):
        member = lax.rem(here[half] + n - d, n)
        ref = group_flat.at[half, :, pl.ds(core * 2, 2), _at(member * rows, rows)]
        return pltpu.make_async_remote_copy(
            src_ref=ref, dst_ref=ref, send_sem=pass_send.at[half, d - 1], recv_sem=pass_recv.at[half, d - 1],
            device_id=_peer("core", 1), device_id_type=MESH)

    def own_copy(half, y):
        src = flat.at[y, :, here[half]] if half == 0 else flat.at[y, here[half]]
        return pltpu.make_async_copy(src, group_flat.at[half, y, :, _at(here[half] * rows, rows)], copy_sem.at[half, y])

    def grad_copy(half, s, d):
        ref = group_grad.at[half, :, _at((here[half] * slots + s) * TREE, TREE)]
        return pltpu.make_async_remote_copy(
            src_ref=ref, dst_ref=ref, send_sem=grad_send.at[half, s, d - 1], recv_sem=grad_recv.at[half, s, d - 1],
            device_id=_peer(axes[half], d), device_id_type=MESH)

    def term_copy(half, d):
        return pltpu.make_async_remote_copy(
            src_ref=term.at[half, d - 1], dst_ref=arrived.at[half, d - 1],
            send_sem=term_send.at[half, d - 1], recv_sem=term_recv.at[half, d - 1],
            device_id=_peer(axes[1 - half], d), device_id_type=MESH)

    def y_copy(half):
        return pltpu.make_async_remote_copy(
            src_ref=across.at[half], dst_ref=landed.at[half], send_sem=y_send.at[half], recv_sem=y_recv.at[half],
            device_id=_peer("y_hi", 1), device_id_type=MESH)

    both = [(half, d) for d in range(1, n) for half in range(2)]

    mp_copy(0).wait_recv()
    mp_copy(2).start()
    for d in range(1, n):
        flat_copy(0, d).start()
    project(4)
    project(5)
    mp_copy(2).wait_recv()
    for d in range(1, n):
        flat_copy(1, d).start()
    for half in range(2):
        for y in range(2):
            own_copy(half, y).start()
    project(6)
    project(7)
    ctx_len = kv.shape[2] - TREE
    q_cols = wq_ref.shape[1]
    qkv[...] = acc[:, :q_cols].astype(BF16)
    for s in range(slots):
        for k in range(2):
            kv[k, s, ctx_len:] = acc[s * TREE:(s + 1) * TREE, q_cols + k * HEAD:q_cols + (k + 1) * HEAD].astype(BF16)
    own_slots.wait()

    def slot_step(s, carry):
        def put_grad(column, block):
            half, at = divmod(column, blocks)
            group_grad[half, at * HEAD:(at + 1) * HEAD, _at((here[half] * slots + s) * TREE, TREE)] = block
        finish(functools.partial(slot_copy, s))
        attend_slot(2, s, len_ref[order_ref[me * slots + s]], qkv, kv, mask_ref, cot_ref, out_ref, bias, put_grad)
        for half, d in both:
            grad_copy(half, s, d).start()
        return carry

    lax.fori_loop(0, slots, slot_step, 0)

    for half, d in both:
        flat_copy(half, d).wait_recv()
        pass_copy(half, d).start()
    for half in range(2):
        for y in range(2):
            own_copy(half, y).wait()
    for half, d in both:
        pass_copy(half, d).wait_recv()
    for s in range(slots):
        for half, d in both:
            grad_copy(half, s, d).wait_recv()

    def product(half, d, y):
        at = lax.rem(here[1 - half] + d, n)
        return _dot(group_grad[half], group_flat[half, y, at], ((1,), (0,)))

    for half, d in both:
        def block_step(y, carry, half=half, d=d):
            term[half, d - 1, y] = product(half, d, y).astype(BF16)
            return carry
        lax.fori_loop(0, 2, block_step, 0)
        term_copy(half, d).start()
    for half in range(2):
        def own_step(y, carry, half=half):
            own[half, y] = product(half, 0, y)
            return carry
        lax.fori_loop(0, 2, own_step, 0)
    for half, d in both:
        term_copy(half, d).wait_recv()

    def total(half, y):
        out = own[half, y]
        for d in range(1, n):
            out += arrived[half, d - 1, y].astype(F32)
        return out

    for half in range(2):
        across[half] = total(half, 1 - y_me).astype(BF16)
        y_copy(half).start()
    for half in range(2):
        own[half, y_me] = total(half, y_me)
    for half in range(2):
        y_copy(half).wait_recv()
        total_t = (own[half, y_me] + landed[half].astype(F32)).T
        for k in range(blocks):
            h = half * blocks + k
            ref, at = (gq_ref, h) if h < q_cols // HEAD else ((gk_ref, gv_ref)[h - q_cols // HEAD], 0)
            ref[:, at * HEAD:(at + 1) * HEAD] = total_t[:, k * HEAD:(k + 1) * HEAD]

    for half, d in both:
        flat_copy(half, d).wait_send()
        pass_copy(half, d).wait_send()
        term_copy(half, d).wait_send()
        for s in range(slots):
            grad_copy(half, s, d).wait_send()
    for half in range(2):
        y_copy(half).wait_send()
    for k in range(3):
        mp_copy(k).wait_send()
    finish_send(spread_copy)
    for s in range(slots):
        finish_send(functools.partial(slot_copy, s))


def local(
    context_kv,
    train_order,
    prompt_lengths,
    parent_nodes,
    tree_mask,
    tree_features,
    query_weight,
    key_weight,
    value_weight,
    cotangent,
):
    slots, _, feat_cols = tree_features.shape
    rows = slots * TREE
    n_y, n, _ = [lax.axis_size(a) for a in WIDE]
    wide = n_y * n * n
    ctx = context_kv.shape[2]
    part = ctx // wide
    width = query_weight.shape[0] // wide
    q_cols = query_weight.shape[1]
    kv_cols = key_weight.shape[1]
    cols = q_cols + 2 * kv_cols
    half_cols = cols // 2
    smem = pl.BlockSpec(memory_space=pltpu.SMEM)
    vmem = pl.BlockSpec(memory_space=pltpu.VMEM)
    hbm = pl.BlockSpec(memory_space=pl.ANY)
    dma = pltpu.SemaphoreType.DMA
    attended, query_gradient, key_gradient, value_gradient = pl.pallas_call(
        train_kernel,
        in_specs=[smem, smem, vmem, vmem, vmem, vmem, hbm, hbm, hbm, hbm],
        out_specs=[vmem] * 4,
        out_shape=[
            jax.ShapeDtypeStruct((rows, q_cols), BF16),
            jax.ShapeDtypeStruct((width, q_cols), F32),
            jax.ShapeDtypeStruct((width, kv_cols), F32),
            jax.ShapeDtypeStruct((width, kv_cols), F32),
        ],
        scratch_shapes=[
            pltpu.VMEM((2, wide * slots, part, HEAD), BF16),
            pltpu.VMEM((2, wide * slots, part, HEAD), BF16),
            pltpu.VMEM((2, slots, ctx + TREE, HEAD), BF16),
            pltpu.VMEM((n_y, n, n, rows, width), BF16),
            pltpu.VMEM((3, n * width, cols), BF16),
            pltpu.VMEM((rows, cols), F32),
            pltpu.VMEM((rows, q_cols), BF16),
            pltpu.VMEM((TREE, ctx + TREE), F32),
            pltpu.VMEM((2, n_y, n, n * rows, width), BF16),
            pltpu.VMEM((2, half_cols, n * rows), BF16),
            pltpu.VMEM((2, n - 1, n_y, half_cols, width), BF16),
            pltpu.VMEM((2, n - 1, n_y, half_cols, width), BF16),
            pltpu.VMEM((2, n_y, half_cols, width), F32),
            pltpu.VMEM((2, half_cols, width), BF16),
            pltpu.VMEM((2, half_cols, width), BF16),
            dma((wide,)), dma((wide,)), dma((slots, wide)), dma((slots, wide)), dma((3,)), dma((3,)), dma((3, 3)),
            dma((2, n - 1)), dma((2, n - 1)), dma((2, n - 1)), dma((2, n - 1)),
            dma((2, slots, n - 1)), dma((2, slots, n - 1)), dma((2, n - 1)), dma((2, n - 1)),
            dma((2,)), dma((2,)), dma((2, 2)),
        ],
        compiler_params=pltpu.CompilerParams(
            collective_id=0, has_side_effects=True, vmem_limit_bytes=63 * 1024 * 1024),
    )(train_order, prompt_lengths, parent_nodes, tree_features, tree_mask, cotangent.reshape(rows, q_cols),
      context_kv, query_weight, key_weight, value_weight)
    return (attended.reshape(slots, TREE, q_cols), query_gradient, key_gradient, value_gradient)


def solution(mesh):
    cube = Mesh(mesh.devices.reshape(2, 4, 4, 2, 2), WIDE + MP)
    return jax.shard_map(
        local,
        mesh=cube,
        in_specs=(
            P(None, WIDE, None, MP),
            P(),
            P(),
            P(WIDE, None),
            P(WIDE, None, None),
            P(WIDE, None, MP),
            P(None, MP),
            P(None, MP),
            P(None, MP),
            P(WIDE, None, MP),
        ),
        out_specs=(P(WIDE, None, MP), P(WIDE, MP), P(WIDE, MP), P(WIDE, MP)),
        check_vma=False,
    )
```

```python
import functools

import jax
import jax.numpy as jnp
from jax import lax
from jax.experimental import pallas as pl
from jax.experimental.pallas import tpu as pltpu
from jax.sharding import Mesh, PartitionSpec as P

HEAD = 128
TREE = 128
F32 = jnp.float32
BF16 = jnp.bfloat16
MESH = pl.DeviceIdType.MESH
WIDE = ("y_hi", "z", "x")
MP = ("y_lo", "core")


def _dot(a, b, dims):
    return lax.dot_general(a, b, (dims, ((), ())), preferred_element_type=F32)


def _peer(axis, step):
    return {axis: lax.rem(lax.axis_index(axis) + step, lax.axis_size(axis))}


def _at(offset, size):
    return pl.ds(pl.multiple_of(offset, size), size)


def attend_slot(chunk, s, length, qkv, kv, mask_ref, cot_ref, out_ref, bias, put_grad):
    scale = HEAD ** (-0.5)
    ctx = kv.shape[2] - TREE
    heads = cot_ref.shape[1] // HEAD
    here = _at(s * TREE, TREE)
    cols = lax.broadcasted_iota(jnp.int32, (TREE, ctx), 1)
    bias[:, :ctx] = jnp.where(cols < length, 0.0, -1e30)
    bias[:, ctx:] = jnp.where(mask_ref[s] == 1, 0.0, -1e30)
    dkey = jnp.zeros((HEAD, TREE), F32)
    dvalue = jnp.zeros((HEAD, TREE), F32)
    for first in range(0, heads, chunk):
        def rows(ref):
            return jnp.concatenate(
                [ref[here, h * HEAD:(h + 1) * HEAD] for h in range(first, first + chunk)], axis=0)
        q = rows(qkv)
        cot = rows(cot_ref)
        score = _dot(q, kv[0, s], ((1,), (1,))) * scale
        score = (score.reshape(chunk, TREE, -1) + bias[...][None]).reshape(chunk * TREE, -1)
        e = jnp.exp(score - jnp.max(score, axis=1, keepdims=True))
        probs = e * (1.0 / jnp.sum(e, axis=1, keepdims=True))
        low = probs.astype(BF16)
        dprob = _dot(cot, kv[1, s], ((1,), (1,)))
        delta = jnp.sum(probs * dprob, axis=1, keepdims=True)
        dscore = ((probs * scale) * (dprob - delta)).astype(BF16)
        out = _dot(low, kv[1, s], ((1,), (0,))).astype(BF16)
        dq = _dot(dscore, kv[0, s], ((1,), (0,)))
        for k in range(chunk):
            h = first + k
            out_ref[here, h * HEAD:(h + 1) * HEAD] = out[k * TREE:(k + 1) * TREE]
            put_grad(h, dq[k * TREE:(k + 1) * TREE].T.astype(BF16))
        dkey += _dot(q, dscore[:, ctx:], ((0,), (0,)))
        dvalue += _dot(cot, low[:, ctx:], ((0,), (0,)))
    put_grad(heads, dkey.astype(BF16))
    put_grad(heads + 1, dvalue.astype(BF16))


def train_kernel(order_ref, len_ref, parent_ref, feat_ref, mask_ref, cot_ref, ctx_ref, wq_ref, wk_ref, wv_ref,
                 out_ref, gq_ref, gk_ref, gv_ref,
                 spread, staged, kv, flat, weight, acc, qkv, bias,
                 group_flat, group_grad, term, arrived, far, far_in, own, across, landed,
                 ctx_send, ctx_recv, slot_send, slot_recv, mp_send, mp_recv, weight_sem,
                 early_send, early_recv, late_send, late_recv, pass_send, pass_recv, grad_send, grad_recv, relay_send, relay_recv, term_send, term_recv, far_send, far_recv,
                 y_send, y_recv, copy_sem):
    axes = ("x", "z")
    n = lax.axis_size("x")
    n_y = lax.axis_size("y_hi")
    wide = n_y * n * n
    slots = mask_ref.shape[0]
    rows = slots * TREE
    width = flat.shape[4]
    part = spread.shape[2]
    half_cols = group_grad.shape[1]
    blocks = half_cols // HEAD
    core = lax.axis_index("core")
    y_lo = lax.axis_index("y_lo")
    here = [lax.axis_index(a) for a in axes]
    y_me = lax.axis_index("y_hi")
    me = (y_me * n + here[1]) * n + here[0]

    steps = [(a, b, c) for a in range(n_y) for b in range(n) for c in range(n)]
    ring = [[lax.rem(here[k] + d, n) for d in range(n)] for k in range(2)]
    y_ring = [y_me, 1 - y_me]
    index = [(y_ring[a] * n + ring[1][b]) * n + ring[0][c] for a, b, c in steps]
    trainer = [{"y_hi": y_ring[a], "z": ring[1][b], "x": ring[0][c]} for a, b, c in steps]

    barrier = pltpu.get_barrier_semaphore()
    for axis in MP:
        pl.semaphore_signal(barrier, inc=1, device_id=_peer(axis, 1), device_id_type=MESH)
    for d in range(1, wide):
        pl.semaphore_signal(barrier, inc=1, device_id=trainer[d], device_id_type=MESH)

    for s in range(slots):
        node = lax.broadcasted_iota(jnp.int32, (TREE, TREE), 0)
        same = node == lax.broadcasted_iota(jnp.int32, (TREE, TREE), 1)
        pick = (node == parent_ref[s:s + 1, :]).astype(F32) + same.astype(F32)
        mixed = _dot(pick.astype(BF16), feat_ref[s], ((0,), (0,))).astype(BF16)
        for k in range(2):
            for x in range(n):
                at = (k * n + x) * width
                flat[y_lo, 2 * core + k, x, s * TREE:(s + 1) * TREE, :] = mixed[:, at:at + width]
    pl.semaphore_wait(barrier, wide + 1)

    def spread_copy(d):
        return pltpu.make_async_remote_copy(
            src_ref=ctx_ref.at[:, :, _at(index[d] * part, part)], dst_ref=spread.at[:, pl.ds(me * slots, slots)],
            send_sem=ctx_send.at[d], recv_sem=ctx_recv.at[d], device_id=trainer[d], device_id_type=MESH)

    def slot_copy(s, d):
        return pltpu.make_async_remote_copy(
            src_ref=staged.at[:, index[d] * slots + s], dst_ref=kv.at[:, s, _at(me * part, part)],
            send_sem=slot_send.at[s, d], recv_sem=slot_recv.at[s, d], device_id=trainer[d], device_id_type=MESH)

    def start(copy):
        for d in range(1, wide):
            copy(d).start()

    def finish(copy):
        for d in range(1, wide):
            copy(d).wait_recv()

    def finish_send(copy):
        for d in range(1, wide):
            copy(d).wait_send()

    own_ctx = pltpu.make_async_copy(
        ctx_ref.at[:, :, _at(me * part, part)], spread.at[:, pl.ds(me * slots, slots)], ctx_recv.at[0])
    start(spread_copy)
    own_ctx.start()

    def shard(a, c, s):
        return flat.at[a, pl.ds(c * 2, 2), :, s * TREE:(s + 1) * TREE]

    def mp_copy(k, s):
        a = (y_lo, y_lo, 1 - y_lo)[k]
        return pltpu.make_async_remote_copy(
            src_ref=shard(a, core, s), dst_ref=shard(a, core, s), send_sem=mp_send.at[k, s], recv_sem=mp_recv.at[k, s],
            device_id=_peer("y_lo" if k == 0 else "core", 1), device_id_type=MESH)

    depth = weight.shape[1]
    buffers = weight.shape[0]
    sources = [(y_lo, core), (y_lo, 1 - core), (1 - y_lo, core), (1 - y_lo, 1 - core)]
    chunks = [(a, 2 * c + k) for a, c in sources for k in range(2)]

    def weight_copies(i):
        a, z = chunks[i]
        at = _at((a * n + z) * depth, depth)
        slot = i % buffers
        q_cols, kv_cols = wq_ref.shape[1], wk_ref.shape[1]
        return [
            pltpu.make_async_copy(wq_ref.at[at], weight.at[slot, :, :q_cols], weight_sem.at[slot, 0]),
            pltpu.make_async_copy(wk_ref.at[at], weight.at[slot, :, q_cols:q_cols + kv_cols], weight_sem.at[slot, 1]),
            pltpu.make_async_copy(wv_ref.at[at], weight.at[slot, :, q_cols + kv_cols:], weight_sem.at[slot, 2]),
        ]

    for i in range(buffers):
        for c in weight_copies(i):
            c.start()

    def early_copy(half, d):
        to = _peer(axes[half], d)
        at = to[axes[half]]
        mine = pl.ds(core * 2, 2)
        return pltpu.make_async_remote_copy(
            src_ref=flat.at[y_lo, mine, at] if half == 0 else flat.at[y_lo, at, mine],
            dst_ref=group_flat.at[half, y_lo, mine, _at(here[half] * rows, rows)],
            send_sem=early_send.at[half, d - 1], recv_sem=early_recv.at[half, d - 1],
            device_id=to, device_id_type=MESH)

    def late_copy(half, s, d):
        to = _peer(axes[half], d)
        at = to[axes[half]]
        mine = pl.ds(core * 2, 2)
        src_rows = pl.ds(s * TREE, TREE)
        return pltpu.make_async_remote_copy(
            src_ref=flat.at[1 - y_lo, mine, at, src_rows] if half == 0 else flat.at[1 - y_lo, at, mine, src_rows],
            dst_ref=group_flat.at[half, 1 - y_lo, mine, _at((here[half] * slots + s) * TREE, TREE)],
            send_sem=late_send.at[half, s, d - 1], recv_sem=late_recv.at[half, s, d - 1],
            device_id=to, device_id_type=MESH)

    def pass_copy(late, half, d):
        a = 1 - y_lo if late else y_lo
        ref = group_flat.at[half, a, pl.ds(core * 2, 2), _at(ring[half][n - d] * rows, rows)]
        return pltpu.make_async_remote_copy(
            src_ref=ref, dst_ref=ref, send_sem=pass_send.at[late, half, d - 1], recv_sem=pass_recv.at[late, half, d - 1],
            device_id=_peer("core", 1), device_id_type=MESH)

    def own_copy(half, y):
        src = flat.at[y, :, here[half]] if half == 0 else flat.at[y, here[half]]
        return pltpu.make_async_copy(src, group_flat.at[half, y, :, _at(here[half] * rows, rows)], copy_sem.at[half, y])

    def grad_copy(half, s, d):
        ref = group_grad.at[half, :, _at((here[half] * slots + s) * TREE, TREE)]
        return pltpu.make_async_remote_copy(
            src_ref=ref, dst_ref=ref, send_sem=grad_send.at[half, s, d // 2], recv_sem=grad_recv.at[half, s, d // 2],
            device_id=_peer(axes[half], d), device_id_type=MESH)

    def relay_copy(half, s, d):
        member = ring[half][n - d]
        mid = half_cols // 2
        ref = group_grad.at[half, pl.ds(0 if d == 1 else mid, mid), _at((member * slots + s) * TREE, TREE)]
        return pltpu.make_async_remote_copy(
            src_ref=ref, dst_ref=ref, send_sem=relay_send.at[half, s, d // 2], recv_sem=relay_recv.at[half, s, d // 2],
            device_id=_peer(axes[half], d), device_id_type=MESH)

    near = [(half, d) for half in range(2) for d in (1, n - 1)]

    def relay(s):
        for half, d in near:
            grad_copy(half, s, d).wait_recv()
            relay_copy(half, s, d).start()

    split = (blocks + 1) // 2 * HEAD
    parts = [(0, split), (split, half_cols)]

    def term_copy(p, half, d):
        cols = pl.ds(parts[p][0], parts[p][1] - parts[p][0])
        return pltpu.make_async_remote_copy(
            src_ref=term.at[half, d // 2, :, cols], dst_ref=arrived.at[half, d // 2, :, cols],
            send_sem=term_send.at[p, half, d // 2], recv_sem=term_recv.at[p, half, d // 2],
            device_id=_peer(axes[1 - half], d), device_id_type=MESH)

    def far_copy(p, half, y):
        cols = pl.ds(parts[p][0], parts[p][1] - parts[p][0])
        return pltpu.make_async_remote_copy(
            src_ref=far.at[half, y, cols], dst_ref=far_in.at[half, y, cols],
            send_sem=far_send.at[p, half, y], recv_sem=far_recv.at[p, half, y],
            device_id=_peer(axes[1 - half], (1, n - 1)[y]), device_id_type=MESH)

    def y_copy(p, half):
        cols = pl.ds(parts[p][0], parts[p][1] - parts[p][0])
        return pltpu.make_async_remote_copy(
            src_ref=across.at[half, cols], dst_ref=landed.at[half, cols],
            send_sem=y_send.at[p, half], recv_sem=y_recv.at[p, half],
            device_id=_peer("y_hi", 1), device_id_type=MESH)

    both = [(half, d) for d in range(1, n) for half in range(2)]

    for k in range(2):
        for s in range(slots):
            mp_copy(k, s).start()
    for d in range(1, n):
        early_copy(0, d).start()

    def project(i):
        a, z = chunks[i]
        for c in weight_copies(i):
            c.wait()
        lhs = jnp.concatenate([flat[a, z, x] for x in range(n)], axis=1)
        product = _dot(lhs, weight[i % buffers], ((1,), (0,)))
        if i == 0:
            acc[...] = product
        else:
            acc[...] += product
        if i + buffers < len(chunks):
            for c in weight_copies(i + buffers):
                c.start()

    project(0)
    project(1)
    for s in range(slots):
        mp_copy(1, s).wait_recv()
    for d in range(1, n):
        early_copy(1, d).start()
    project(2)
    project(3)

    finish(spread_copy)
    own_ctx.wait()

    def place(r, carry):
        staged[:, r] = spread[:, order_ref[r]]
        return carry

    lax.fori_loop(0, wide * slots, place, 0)
    for s in range(slots):
        start(functools.partial(slot_copy, s))
    own_slots = pltpu.make_async_copy(
        staged.at[:, pl.ds(me * slots, slots)], kv.at[:, :, _at(me * part, part)], slot_recv.at[0, 0])
    own_slots.start()

    def sibling_arrived(s):
        mp_copy(2, s).wait_recv()
        for d in range(1, n):
            late_copy(1, s, d).start()

    for s in range(slots):
        mp_copy(0, s).wait_recv()
        mp_copy(2, s).start()
        for d in range(1, n):
            late_copy(0, s, d).start()
        if s > 0:
            sibling_arrived(s - 1)
        if s == 1:
            for half, d in both:
                early_copy(half, d).wait_recv()
                pass_copy(0, half, d).start()
    project(4)
    project(5)
    sibling_arrived(slots - 1)
    for half in range(2):
        for y in range(2):
            own_copy(half, y).start()
    project(6)
    project(7)
    ctx_len = kv.shape[2] - TREE
    q_cols = wq_ref.shape[1]
    qkv[...] = acc[:, :q_cols].astype(BF16)
    for s in range(slots):
        for k in range(2):
            kv[k, s, ctx_len:] = acc[s * TREE:(s + 1) * TREE, q_cols + k * HEAD:q_cols + (k + 1) * HEAD].astype(BF16)
    own_slots.wait()

    def slot_step(s, carry):
        def put_grad(column, block):
            half, at = divmod(column, blocks)
            group_grad[half, at * HEAD:(at + 1) * HEAD, _at((here[half] * slots + s) * TREE, TREE)] = block
        @pl.when(s == slots - 1)
        def _():
            for half, d in both:
                for k in range(slots):
                    late_copy(half, k, d).wait_recv()
                pass_copy(1, half, d).start()
        finish(functools.partial(slot_copy, s))
        attend_slot(2, s, len_ref[order_ref[me * slots + s]], qkv, kv, mask_ref, cot_ref, out_ref, bias, put_grad)
        for half, d in near:
            grad_copy(half, s, d).start()

        @pl.when(s > 0)
        def _():
            relay(s - 1)
        return carry

    lax.fori_loop(0, slots, slot_step, 0)
    relay(slots - 1)

    for half in range(2):
        for y in range(2):
            own_copy(half, y).wait()
    for late in range(2):
        for half, d in both:
            pass_copy(late, half, d).wait_recv()
    for s in range(slots):
        for half, d in near:
            relay_copy(half, s, d).wait_recv()

    def product(p, half, d, y):
        lo, hi = parts[p]
        return _dot(group_grad[half, lo:hi], group_flat[half, y, ring[1 - half][d]], ((1,), (0,)))

    for p, (lo, hi) in enumerate(parts):
        for half in range(2):
            for y in range(n_y):
                far[half, y, lo:hi] = product(p, half, 2, y).astype(BF16)
                far_copy(p, half, y).start()
    for p, (lo, hi) in enumerate(parts):
        for half in range(2):
            for y in range(n_y):
                own[half, y, lo:hi] = product(p, half, 0, y)
        for half, d in near:
            y = d // 2
            term[half, d // 2, 1 - y, lo:hi] = product(p, half, d, 1 - y).astype(BF16)
            far_copy(p, half, y).wait_recv()
            term[half, d // 2, y, lo:hi] = (product(p, half, d, y) + far_in[half, y, lo:hi].astype(F32)).astype(BF16)
            term_copy(p, half, d).start()

    def total(p, half, y):
        lo, hi = parts[p]
        out = own[half, y, lo:hi]
        for k in range(2):
            out += arrived[half, k, y, lo:hi].astype(F32)
        return out

    for p, (lo, hi) in enumerate(parts):
        for half in range(2):
            for d in (1, n - 1):
                term_copy(p, half, d).wait_recv()
            across[half, lo:hi] = total(p, half, 1 - y_me).astype(BF16)
            y_copy(p, half).start()
        for half in range(2):
            own[half, y_me, lo:hi] = total(p, half, y_me)
    for p, (lo, hi) in enumerate(parts):
        for half in range(2):
            y_copy(p, half).wait_recv()
            final = (own[half, y_me, lo:hi] + landed[half, lo:hi].astype(F32)).T
            for k in range(lo // HEAD, hi // HEAD):
                h = half * blocks + k
                ref, at = (gq_ref, h) if h < q_cols // HEAD else ((gk_ref, gv_ref)[h - q_cols // HEAD], 0)
                ref[:, at * HEAD:(at + 1) * HEAD] = final[:, k * HEAD - lo:(k + 1) * HEAD - lo]

    for half, d in both:
        early_copy(half, d).wait_send()
        for k in range(2):
            pass_copy(k, half, d).wait_send()
        for s in range(slots):
            late_copy(half, s, d).wait_send()
    for half, d in near:
        for p in range(2):
            term_copy(p, half, d).wait_send()
            far_copy(p, half, d // 2).wait_send()
        for s in range(slots):
            grad_copy(half, s, d).wait_send()
            relay_copy(half, s, d).wait_send()
    for p in range(2):
        for half in range(2):
            y_copy(p, half).wait_send()
    for k in range(3):
        for s in range(slots):
            mp_copy(k, s).wait_send()
    finish_send(spread_copy)
    for s in range(slots):
        finish_send(functools.partial(slot_copy, s))


def local(
    context_kv,
    train_order,
    prompt_lengths,
    parent_nodes,
    tree_mask,
    tree_features,
    query_weight,
    key_weight,
    value_weight,
    cotangent,
):
    slots, _, feat_cols = tree_features.shape
    rows = slots * TREE
    n_y, n, _ = [lax.axis_size(a) for a in WIDE]
    wide = n_y * n * n
    ctx = context_kv.shape[2]
    part = ctx // wide
    width = query_weight.shape[0] // wide
    q_cols = query_weight.shape[1]
    kv_cols = key_weight.shape[1]
    cols = q_cols + 2 * kv_cols
    half_cols = cols // 2
    smem = pl.BlockSpec(memory_space=pltpu.SMEM)
    vmem = pl.BlockSpec(memory_space=pltpu.VMEM)
    hbm = pl.BlockSpec(memory_space=pl.ANY)
    dma = pltpu.SemaphoreType.DMA
    attended, query_gradient, key_gradient, value_gradient = pl.pallas_call(
        train_kernel,
        in_specs=[smem, smem, vmem, vmem, vmem, vmem, hbm, hbm, hbm, hbm],
        out_specs=[vmem] * 4,
        out_shape=[
            jax.ShapeDtypeStruct((rows, q_cols), BF16),
            jax.ShapeDtypeStruct((width, q_cols), F32),
            jax.ShapeDtypeStruct((width, kv_cols), F32),
            jax.ShapeDtypeStruct((width, kv_cols), F32),
        ],
        scratch_shapes=[
            pltpu.VMEM((2, wide * slots, part, HEAD), BF16),
            pltpu.VMEM((2, wide * slots, part, HEAD), BF16),
            pltpu.VMEM((2, slots, ctx + TREE, HEAD), BF16),
            pltpu.VMEM((n_y, n, n, rows, width), BF16),
            pltpu.VMEM((3, n * width, cols), BF16),
            pltpu.VMEM((rows, cols), F32),
            pltpu.VMEM((rows, q_cols), BF16),
            pltpu.VMEM((TREE, ctx + TREE), F32),
            pltpu.VMEM((2, n_y, n, n * rows, width), BF16),
            pltpu.VMEM((2, half_cols, n * rows), BF16),
            pltpu.VMEM((2, 2, n_y, half_cols, width), BF16),
            pltpu.VMEM((2, 2, n_y, half_cols, width), BF16),
            pltpu.VMEM((2, n_y, half_cols, width), BF16),
            pltpu.VMEM((2, n_y, half_cols, width), BF16),
            pltpu.VMEM((2, n_y, half_cols, width), F32),
            pltpu.VMEM((2, half_cols, width), BF16),
            pltpu.VMEM((2, half_cols, width), BF16),
            dma((wide,)), dma((wide,)), dma((slots, wide)), dma((slots, wide)),
            dma((3, slots)), dma((3, slots)), dma((3, 3)),
            dma((2, n - 1)), dma((2, n - 1)), dma((2, slots, n - 1)), dma((2, slots, n - 1)),
            dma((2, 2, n - 1)), dma((2, 2, n - 1)),
            dma((2, slots, 2)), dma((2, slots, 2)), dma((2, slots, 2)), dma((2, slots, 2)),
            dma((2, 2, 2)), dma((2, 2, 2)), dma((2, 2, 2)), dma((2, 2, 2)),
            dma((2, 2)), dma((2, 2)), dma((2, 2)),
        ],
        compiler_params=pltpu.CompilerParams(
            collective_id=0, has_side_effects=True, vmem_limit_bytes=63 * 1024 * 1024),
    )(train_order, prompt_lengths, parent_nodes, tree_features, tree_mask, cotangent.reshape(rows, q_cols),
      context_kv, query_weight, key_weight, value_weight)
    return (attended.reshape(slots, TREE, q_cols), query_gradient, key_gradient, value_gradient)


def solution(mesh):
    cube = Mesh(mesh.devices.reshape(2, 4, 4, 2, 2), WIDE + MP)
    return jax.shard_map(
        local,
        mesh=cube,
        in_specs=(
            P(None, WIDE, None, MP),
            P(),
            P(),
            P(WIDE, None),
            P(WIDE, None, None),
            P(WIDE, None, MP),
            P(None, MP),
            P(None, MP),
            P(None, MP),
            P(WIDE, None, MP),
        ),
        out_specs=(P(WIDE, None, MP), P(WIDE, MP), P(WIDE, MP), P(WIDE, MP)),
        check_vma=False,
    )
```

```python
import functools

import jax
import jax.numpy as jnp
from jax import lax
from jax.experimental import pallas as pl
from jax.experimental.pallas import tpu as pltpu
from jax.sharding import Mesh, PartitionSpec as P

HEAD = 128
TREE = 128
F32 = jnp.float32
BF16 = jnp.bfloat16
MESH = pl.DeviceIdType.MESH
WIDE = ("y_hi", "z", "x")
MP = ("y_lo", "core")


def _dot(a, b, dims):
    return lax.dot_general(a, b, (dims, ((), ())), preferred_element_type=F32)


def _peer(axis, step):
    return {axis: lax.rem(lax.axis_index(axis) + step, lax.axis_size(axis))}


def _at(offset, size):
    return pl.ds(pl.multiple_of(offset, size), size)


def attend_slot(chunk, s, length, qkv, kv, mask_ref, cot_ref, out_ref, bias, put_grad):
    scale = HEAD ** (-0.5)
    ctx = kv.shape[2] - TREE
    heads = cot_ref.shape[1] // HEAD
    here = _at(s * TREE, TREE)
    cols = lax.broadcasted_iota(jnp.int32, (TREE, ctx), 1)
    bias[:, :ctx] = jnp.where(cols < length, 0.0, -1e30)
    bias[:, ctx:] = jnp.where(mask_ref[s] == 1, 0.0, -1e30)
    dkey = jnp.zeros((HEAD, TREE), F32)
    dvalue = jnp.zeros((HEAD, TREE), F32)
    for first in range(0, heads, chunk):
        def rows(ref):
            return jnp.concatenate(
                [ref[here, h * HEAD:(h + 1) * HEAD] for h in range(first, first + chunk)], axis=0)
        q = rows(qkv)
        cot = rows(cot_ref)
        score = _dot(q, kv[0, s], ((1,), (1,))) * scale
        score = (score.reshape(chunk, TREE, -1) + bias[...][None]).reshape(chunk * TREE, -1)
        e = jnp.exp(score - jnp.max(score, axis=1, keepdims=True))
        probs = e * (1.0 / jnp.sum(e, axis=1, keepdims=True))
        low = probs.astype(BF16)
        dprob = _dot(cot, kv[1, s], ((1,), (1,)))
        delta = jnp.sum(probs * dprob, axis=1, keepdims=True)
        dscore = ((probs * scale) * (dprob - delta)).astype(BF16)
        out = _dot(low, kv[1, s], ((1,), (0,))).astype(BF16)
        dq = _dot(dscore, kv[0, s], ((1,), (0,)))
        for k in range(chunk):
            h = first + k
            out_ref[here, h * HEAD:(h + 1) * HEAD] = out[k * TREE:(k + 1) * TREE]
            put_grad(h, dq[k * TREE:(k + 1) * TREE].T.astype(BF16))
        dkey += _dot(q, dscore[:, ctx:], ((0,), (0,)))
        dvalue += _dot(cot, low[:, ctx:], ((0,), (0,)))
    put_grad(heads, dkey.astype(BF16))
    put_grad(heads + 1, dvalue.astype(BF16))


def train_kernel(order_ref, len_ref, parent_ref, feat_ref, mask_ref, cot_ref, ctx_ref, wq_ref, wk_ref, wv_ref,
                 out_ref, gq_ref, gk_ref, gv_ref,
                 spread, staged, kv, flat, weight, acc, qkv, bias,
                 group_flat, group_grad, term, arrived, far, far_in, own, across, landed,
                 ctx_send, ctx_recv, slot_send, slot_recv, mp_send, mp_recv, weight_sem,
                 early_send, early_recv, late_send, late_recv, pass_send, pass_recv, grad_send, grad_recv, relay_send, relay_recv, term_send, term_recv, far_send, far_recv,
                 y_send, y_recv, copy_sem, plane_in, all_in):
    axes = ("x", "z")
    n = lax.axis_size("x")
    n_y = lax.axis_size("y_hi")
    wide = n_y * n * n
    slots = mask_ref.shape[0]
    rows = slots * TREE
    width = flat.shape[4]
    part = spread.shape[2]
    half_cols = group_grad.shape[1]
    blocks = half_cols // HEAD
    core = lax.axis_index("core")
    y_lo = lax.axis_index("y_lo")
    here = [lax.axis_index(a) for a in axes]
    y_me = lax.axis_index("y_hi")
    me = (y_me * n + here[1]) * n + here[0]

    steps = [(a, b, c) for a in range(n_y) for b in range(n) for c in range(n)]
    ring = [[lax.rem(here[k] + d, n) for d in range(n)] for k in range(2)]
    y_ring = [y_me, 1 - y_me]
    index = [(y_ring[a] * n + ring[1][b]) * n + ring[0][c] for a, b, c in steps]
    trainer = [{"y_hi": y_ring[a], "z": ring[1][b], "x": ring[0][c]} for a, b, c in steps]

    plane = n * n
    in_row, in_column = range(1, n), range(n, plane, n)
    barrier = pltpu.get_barrier_semaphore()
    for axis in MP:
        pl.semaphore_signal(barrier, inc=1, device_id=_peer(axis, 1), device_id_type=MESH)
    for d in (plane, *in_row, *in_column):
        pl.semaphore_signal(barrier, inc=1, device_id=trainer[d], device_id_type=MESH)

    def shard(a, c, s):
        return flat.at[a, pl.ds(c * 2, 2), :, s * TREE:(s + 1) * TREE]

    def mp_copy(k, s):
        a = (y_lo, y_lo, 1 - y_lo)[k]
        return pltpu.make_async_remote_copy(
            src_ref=shard(a, core, s), dst_ref=shard(a, core, s), send_sem=mp_send.at[k, s], recv_sem=mp_recv.at[k, s],
            device_id=_peer("y_lo" if k == 0 else "core", 1), device_id_type=MESH)

    for s in range(slots):
        node = lax.broadcasted_iota(jnp.int32, (TREE, TREE), 0)
        same = node == lax.broadcasted_iota(jnp.int32, (TREE, TREE), 1)
        pick = (node == parent_ref[s:s + 1, :]).astype(F32) + same.astype(F32)
        mixed = _dot(pick.astype(BF16), feat_ref[s], ((0,), (0,))).astype(BF16)
        for k in range(2):
            for x in range(n):
                at = (k * n + x) * width
                flat[y_lo, 2 * core + k, x, s * TREE:(s + 1) * TREE, :] = mixed[:, at:at + width]
    pl.semaphore_wait(barrier, 2 * n + 1)
    for d in in_column:
        pl.semaphore_signal(plane_in, inc=1, device_id=trainer[d], device_id_type=MESH)

    def spread_copy(d):
        return pltpu.make_async_remote_copy(
            src_ref=ctx_ref.at[:, :, _at(index[d] * part, part)], dst_ref=spread.at[:, pl.ds(me * slots, slots)],
            send_sem=ctx_send.at[d], recv_sem=ctx_recv.at[d], device_id=trainer[d], device_id_type=MESH)

    def plane_copy(d):
        return pltpu.make_async_remote_copy(
            src_ref=staged.at[:, pl.ds(index[d] * slots, slots)], dst_ref=kv.at[:, :, _at(me * part, part)],
            send_sem=slot_send.at[slots, d], recv_sem=slot_recv.at[slots, d],
            device_id=trainer[d], device_id_type=MESH)

    def cross_copy(s, d):
        return pltpu.make_async_remote_copy(
            src_ref=staged.at[:, index[d] * slots + s], dst_ref=kv.at[:, s, _at(me * part, part)],
            send_sem=slot_send.at[s, d - plane], recv_sem=slot_recv.at[s, d - plane],
            device_id=trainer[d], device_id_type=MESH)

    def start_cross(s):
        for d in range(plane, wide):
            cross_copy(s, d).start()

    own_ctx = pltpu.make_async_copy(
        ctx_ref.at[:, :, _at(me * part, part)], spread.at[:, pl.ds(me * slots, slots)], ctx_recv.at[0])
    for k in range(2):
        for s in range(1 if k == 0 else slots):
            mp_copy(k, s).start()
    for d in (plane, *in_row, *in_column):
        spread_copy(d).start()
    own_ctx.start()
    pl.semaphore_wait(plane_in, n - 1)
    pl.semaphore_signal(all_in, inc=1, device_id=trainer[plane], device_id_type=MESH)
    for d in range(1, plane):
        if d not in in_row and d not in in_column:
            spread_copy(d).start()
    pl.semaphore_wait(all_in, 1)
    for d in range(plane + 1, wide):
        spread_copy(d).start()

    depth = weight.shape[1]
    buffers = weight.shape[0]
    sources = [(y_lo, core), (y_lo, 1 - core), (1 - y_lo, core), (1 - y_lo, 1 - core)]
    chunks = [(a, 2 * c + k) for a, c in sources for k in range(2)]

    def weight_copies(i):
        a, z = chunks[i]
        at = _at((a * n + z) * depth, depth)
        slot = i % buffers
        q_cols, kv_cols = wq_ref.shape[1], wk_ref.shape[1]
        return [
            pltpu.make_async_copy(wq_ref.at[at], weight.at[slot, :, :q_cols], weight_sem.at[slot, 0]),
            pltpu.make_async_copy(wk_ref.at[at], weight.at[slot, :, q_cols:q_cols + kv_cols], weight_sem.at[slot, 1]),
            pltpu.make_async_copy(wv_ref.at[at], weight.at[slot, :, q_cols + kv_cols:], weight_sem.at[slot, 2]),
        ]

    for i in range(buffers):
        for c in weight_copies(i):
            c.start()

    def early_copy(half, d):
        to = _peer(axes[half], d)
        at = to[axes[half]]
        mine = pl.ds(core * 2, 2)
        return pltpu.make_async_remote_copy(
            src_ref=flat.at[y_lo, mine, at] if half == 0 else flat.at[y_lo, at, mine],
            dst_ref=group_flat.at[half, y_lo, mine, _at(here[half] * rows, rows)],
            send_sem=early_send.at[half, d - 1], recv_sem=early_recv.at[half, d - 1],
            device_id=to, device_id_type=MESH)

    def late_copy(half, s, d):
        to = _peer(axes[half], d)
        at = to[axes[half]]
        mine = pl.ds(core * 2, 2)
        src_rows = pl.ds(s * TREE, TREE)
        return pltpu.make_async_remote_copy(
            src_ref=flat.at[1 - y_lo, mine, at, src_rows] if half == 0 else flat.at[1 - y_lo, at, mine, src_rows],
            dst_ref=group_flat.at[half, 1 - y_lo, mine, _at((here[half] * slots + s) * TREE, TREE)],
            send_sem=late_send.at[half, s, d - 1], recv_sem=late_recv.at[half, s, d - 1],
            device_id=to, device_id_type=MESH)

    def pass_copy(late, half, d):
        a = 1 - y_lo if late else y_lo
        ref = group_flat.at[half, a, pl.ds(core * 2, 2), _at(ring[half][n - d] * rows, rows)]
        return pltpu.make_async_remote_copy(
            src_ref=ref, dst_ref=ref, send_sem=pass_send.at[late, half, d - 1], recv_sem=pass_recv.at[late, half, d - 1],
            device_id=_peer("core", 1), device_id_type=MESH)

    def own_copy(half, y):
        src = flat.at[y, :, here[half]] if half == 0 else flat.at[y, here[half]]
        return pltpu.make_async_copy(src, group_flat.at[half, y, :, _at(here[half] * rows, rows)], copy_sem.at[half, y])

    def grad_copy(half, s, d):
        ref = group_grad.at[half, :, _at((here[half] * slots + s) * TREE, TREE)]
        return pltpu.make_async_remote_copy(
            src_ref=ref, dst_ref=ref, send_sem=grad_send.at[half, s, d // 2], recv_sem=grad_recv.at[half, s, d // 2],
            device_id=_peer(axes[half], d), device_id_type=MESH)

    def relay_copy(half, s, d):
        member = ring[half][n - d]
        mid = half_cols // 2
        ref = group_grad.at[half, pl.ds(0 if d == 1 else mid, mid), _at((member * slots + s) * TREE, TREE)]
        return pltpu.make_async_remote_copy(
            src_ref=ref, dst_ref=ref, send_sem=relay_send.at[half, s, d // 2], recv_sem=relay_recv.at[half, s, d // 2],
            device_id=_peer(axes[half], d), device_id_type=MESH)

    near = [(half, d) for half in range(2) for d in (1, n - 1)]

    def relay(s):
        for half, d in near:
            grad_copy(half, s, d).wait_recv()
            relay_copy(half, s, d).start()

    split = (blocks + 1) // 2 * HEAD
    parts = [(0, split), (split, half_cols)]

    def term_copy(p, half, d):
        cols = pl.ds(parts[p][0], parts[p][1] - parts[p][0])
        return pltpu.make_async_remote_copy(
            src_ref=term.at[half, d // 2, :, cols], dst_ref=arrived.at[half, d // 2, :, cols],
            send_sem=term_send.at[p, half, d // 2], recv_sem=term_recv.at[p, half, d // 2],
            device_id=_peer(axes[1 - half], d), device_id_type=MESH)

    def far_copy(p, half, y):
        cols = pl.ds(parts[p][0], parts[p][1] - parts[p][0])
        return pltpu.make_async_remote_copy(
            src_ref=far.at[half, y, cols], dst_ref=far_in.at[half, y, cols],
            send_sem=far_send.at[p, half, y], recv_sem=far_recv.at[p, half, y],
            device_id=_peer(axes[1 - half], (1, n - 1)[y]), device_id_type=MESH)

    def y_copy(p, half):
        cols = pl.ds(parts[p][0], parts[p][1] - parts[p][0])
        return pltpu.make_async_remote_copy(
            src_ref=across.at[half, cols], dst_ref=landed.at[half, cols],
            send_sem=y_send.at[p, half], recv_sem=y_recv.at[p, half],
            device_id=_peer("y_hi", 1), device_id_type=MESH)

    both = [(half, d) for d in range(1, n) for half in range(2)]


    def project(i):
        a, z = chunks[i]
        for c in weight_copies(i):
            c.wait()
        lhs = jnp.concatenate([flat[a, z, x] for x in range(n)], axis=1)
        product = _dot(lhs, weight[i % buffers], ((1,), (0,)))
        if i == 0:
            acc[...] = product
        else:
            acc[...] += product
        if i + buffers < len(chunks):
            for c in weight_copies(i + buffers):
                c.start()

    for d in range(1, n):
        early_copy(0, d).start()
    project(0)
    project(1)
    for s in range(slots):
        mp_copy(1, s).wait_recv()
    for d in range(1, n):
        early_copy(1, d).start()
    project(2)
    project(3)

    for d in range(1, wide):
        spread_copy(d).wait_recv()
    own_ctx.wait()
    for s in range(1, slots):
        mp_copy(0, s).start()

    def place(r, carry):
        staged[:, r] = spread[:, order_ref[r]]
        return carry

    lax.fori_loop(0, wide * slots, place, 0)
    for d in range(1, plane):
        plane_copy(d).start()
    own_slots = pltpu.make_async_copy(
        staged.at[:, pl.ds(me * slots, slots)], kv.at[:, :, _at(me * part, part)], copy_sem.at[2, 0])
    own_slots.start()

    def sibling_arrived(s):
        mp_copy(2, s).wait_recv()
        for d in range(1, n):
            late_copy(1, s, d).start()

    for s in range(slots):
        mp_copy(0, s).wait_recv()
        mp_copy(2, s).start()
        for d in range(1, n):
            late_copy(0, s, d).start()
        if s > 0:
            start_cross(s - 1)
            sibling_arrived(s - 1)
        if s == slots - 1:
            for half, d in both:
                early_copy(half, d).wait_recv()
                pass_copy(0, half, d).start()
    project(4)
    project(5)
    start_cross(slots - 1)
    sibling_arrived(slots - 1)
    for half in range(2):
        for y in range(2):
            own_copy(half, y).start()
    project(6)
    project(7)
    ctx_len = kv.shape[2] - TREE
    q_cols = wq_ref.shape[1]
    qkv[...] = acc[:, :q_cols].astype(BF16)
    for s in range(slots):
        for k in range(2):
            kv[k, s, ctx_len:] = acc[s * TREE:(s + 1) * TREE, q_cols + k * HEAD:q_cols + (k + 1) * HEAD].astype(BF16)
    own_slots.wait()
    for d in range(1, plane):
        plane_copy(d).wait_recv()

    def slot_step(s, carry):
        def put_grad(column, block):
            half, at = divmod(column, blocks)
            group_grad[half, at * HEAD:(at + 1) * HEAD, _at((here[half] * slots + s) * TREE, TREE)] = block
        @pl.when(s == slots - 1)
        def _():
            for half, d in both:
                for k in range(slots):
                    late_copy(half, k, d).wait_recv()
                pass_copy(1, half, d).start()
        for d in range(plane, wide):
            cross_copy(s, d).wait_recv()
        attend_slot(2, s, len_ref[order_ref[me * slots + s]], qkv, kv, mask_ref, cot_ref, out_ref, bias, put_grad)
        for half, d in near:
            grad_copy(half, s, d).start()

        @pl.when(s > 0)
        def _():
            relay(s - 1)
        return carry

    lax.fori_loop(0, slots, slot_step, 0)
    relay(slots - 1)

    for half in range(2):
        for y in range(2):
            own_copy(half, y).wait()
    for late in range(2):
        for half, d in both:
            pass_copy(late, half, d).wait_recv()
    for s in range(slots):
        for half, d in near:
            relay_copy(half, s, d).wait_recv()

    def product(p, half, d, y):
        lo, hi = parts[p]
        return _dot(group_grad[half, lo:hi], group_flat[half, y, ring[1 - half][d]], ((1,), (0,)))

    for p, (lo, hi) in enumerate(parts):
        for half in range(2):
            for y in range(n_y):
                far[half, y, lo:hi] = product(p, half, 2, y).astype(BF16)
                far_copy(p, half, y).start()
    for p, (lo, hi) in enumerate(parts):
        for half in range(2):
            for y in range(n_y):
                own[half, y, lo:hi] = product(p, half, 0, y)
        for half, d in near:
            y = d // 2
            term[half, d // 2, 1 - y, lo:hi] = product(p, half, d, 1 - y).astype(BF16)
            far_copy(p, half, y).wait_recv()
            term[half, d // 2, y, lo:hi] = (product(p, half, d, y) + far_in[half, y, lo:hi].astype(F32)).astype(BF16)
            term_copy(p, half, d).start()

    def total(p, half, y):
        lo, hi = parts[p]
        out = own[half, y, lo:hi]
        for k in range(2):
            out += arrived[half, k, y, lo:hi].astype(F32)
        return out

    for p, (lo, hi) in enumerate(parts):
        for half in range(2):
            for d in (1, n - 1):
                term_copy(p, half, d).wait_recv()
            across[half, lo:hi] = total(p, half, 1 - y_me).astype(BF16)
            y_copy(p, half).start()
        for half in range(2):
            own[half, y_me, lo:hi] = total(p, half, y_me)
    for p, (lo, hi) in enumerate(parts):
        for half in range(2):
            y_copy(p, half).wait_recv()
            final = (own[half, y_me, lo:hi] + landed[half, lo:hi].astype(F32)).T
            for k in range(lo // HEAD, hi // HEAD):
                h = half * blocks + k
                ref, at = (gq_ref, h) if h < q_cols // HEAD else ((gk_ref, gv_ref)[h - q_cols // HEAD], 0)
                ref[:, at * HEAD:(at + 1) * HEAD] = final[:, k * HEAD - lo:(k + 1) * HEAD - lo]

    for half, d in both:
        early_copy(half, d).wait_send()
        for k in range(2):
            pass_copy(k, half, d).wait_send()
        for s in range(slots):
            late_copy(half, s, d).wait_send()
    for half, d in near:
        for p in range(2):
            term_copy(p, half, d).wait_send()
            far_copy(p, half, d // 2).wait_send()
        for s in range(slots):
            grad_copy(half, s, d).wait_send()
            relay_copy(half, s, d).wait_send()
    for p in range(2):
        for half in range(2):
            y_copy(p, half).wait_send()
    for k in range(3):
        for s in range(slots):
            mp_copy(k, s).wait_send()
    for d in range(1, wide):
        spread_copy(d).wait_send()
    for d in range(1, plane):
        plane_copy(d).wait_send()
    for s in range(slots):
        for d in range(plane, wide):
            cross_copy(s, d).wait_send()


def hand_on_kernel(*refs):
    n = len(refs) // 2
    for k in range(n):
        refs[n + k][...] = refs[k][...]


def hand_on(arrays):
    vmem = pl.BlockSpec(memory_space=pltpu.VMEM)
    return pl.pallas_call(
        hand_on_kernel,
        in_specs=[vmem] * len(arrays),
        out_specs=[vmem] * len(arrays),
        out_shape=[jax.ShapeDtypeStruct(a.shape, a.dtype) for a in arrays],
    )(*arrays)


def local(
    context_kv,
    train_order,
    prompt_lengths,
    parent_nodes,
    tree_mask,
    tree_features,
    query_weight,
    key_weight,
    value_weight,
    cotangent,
):
    slots, _, feat_cols = tree_features.shape
    rows = slots * TREE
    n_y, n, _ = [lax.axis_size(a) for a in WIDE]
    wide = n_y * n * n
    ctx = context_kv.shape[2]
    part = ctx // wide
    width = query_weight.shape[0] // wide
    q_cols = query_weight.shape[1]
    kv_cols = key_weight.shape[1]
    cols = q_cols + 2 * kv_cols
    half_cols = cols // 2
    smem = pl.BlockSpec(memory_space=pltpu.SMEM)
    vmem = pl.BlockSpec(memory_space=pltpu.VMEM)
    hbm = pl.BlockSpec(memory_space=pl.ANY)
    dma = pltpu.SemaphoreType.DMA
    results = pl.pallas_call(
        train_kernel,
        in_specs=[smem, smem, vmem, vmem, vmem, vmem, hbm, hbm, hbm, hbm],
        out_specs=[vmem] * 4,
        out_shape=[
            jax.ShapeDtypeStruct((rows, q_cols), BF16),
            jax.ShapeDtypeStruct((width, q_cols), F32),
            jax.ShapeDtypeStruct((width, kv_cols), F32),
            jax.ShapeDtypeStruct((width, kv_cols), F32),
        ],
        scratch_shapes=[
            pltpu.VMEM((2, wide * slots, part, HEAD), BF16),
            pltpu.VMEM((2, wide * slots, part, HEAD), BF16),
            pltpu.VMEM((2, slots, ctx + TREE, HEAD), BF16),
            pltpu.VMEM((n_y, n, n, rows, width), BF16),
            pltpu.VMEM((3, n * width, cols), BF16),
            pltpu.VMEM((rows, cols), F32),
            pltpu.VMEM((rows, q_cols), BF16),
            pltpu.VMEM((TREE, ctx + TREE), F32),
            pltpu.VMEM((2, n_y, n, n * rows, width), BF16),
            pltpu.VMEM((2, half_cols, n * rows), BF16),
            pltpu.VMEM((2, 2, n_y, half_cols, width), BF16),
            pltpu.VMEM((2, 2, n_y, half_cols, width), BF16),
            pltpu.VMEM((2, n_y, half_cols, width), BF16),
            pltpu.VMEM((2, n_y, half_cols, width), BF16),
            pltpu.VMEM((2, n_y, half_cols, width), F32),
            pltpu.VMEM((2, half_cols, width), BF16),
            pltpu.VMEM((2, half_cols, width), BF16),
            dma((wide,)), dma((wide,)), dma((slots + 1, n * n)), dma((slots + 1, n * n)),
            dma((3, slots)), dma((3, slots)), dma((3, 3)),
            dma((2, n - 1)), dma((2, n - 1)), dma((2, slots, n - 1)), dma((2, slots, n - 1)),
            dma((2, 2, n - 1)), dma((2, 2, n - 1)),
            dma((2, slots, 2)), dma((2, slots, 2)), dma((2, slots, 2)), dma((2, slots, 2)),
            dma((2, 2, 2)), dma((2, 2, 2)), dma((2, 2, 2)), dma((2, 2, 2)),
            dma((2, 2)), dma((2, 2)), dma((3, 2)), pltpu.SemaphoreType.REGULAR, pltpu.SemaphoreType.REGULAR,
        ],
        compiler_params=pltpu.CompilerParams(
            collective_id=0, has_side_effects=True, vmem_limit_bytes=63 * 1024 * 1024),
    )(train_order, prompt_lengths, parent_nodes, tree_features, tree_mask, cotangent.reshape(rows, q_cols),
      context_kv, query_weight, key_weight, value_weight)
    attended, query_gradient, key_gradient, value_gradient = hand_on(results)
    return (attended.reshape(slots, TREE, q_cols), query_gradient, key_gradient, value_gradient)


def solution(mesh):
    cube = Mesh(mesh.devices.reshape(2, 4, 4, 2, 2), WIDE + MP)
    return jax.shard_map(
        local,
        mesh=cube,
        in_specs=(
            P(None, WIDE, None, MP),
            P(),
            P(),
            P(WIDE, None),
            P(WIDE, None, None),
            P(WIDE, None, MP),
            P(None, MP),
            P(None, MP),
            P(None, MP),
            P(WIDE, None, MP),
        ),
        out_specs=(P(WIDE, None, MP), P(WIDE, MP), P(WIDE, MP), P(WIDE, MP)),
        check_vma=False,
    )
```

```python
import functools

import jax
import jax.numpy as jnp
from jax import lax
from jax.experimental import pallas as pl
from jax.experimental.pallas import tpu as pltpu
from jax.sharding import Mesh, PartitionSpec as P

HEAD = 128
TREE = 128
F32 = jnp.float32
BF16 = jnp.bfloat16
MESH = pl.DeviceIdType.MESH
WIDE = ("y_hi", "z", "x")
MP = ("y_lo", "core")


def _dot(a, b, dims):
    return lax.dot_general(a, b, (dims, ((), ())), preferred_element_type=F32)


def _peer(axis, step):
    return {axis: lax.rem(lax.axis_index(axis) + step, lax.axis_size(axis))}


def _at(offset, size):
    return pl.ds(pl.multiple_of(offset, size), size)


def attend_slot(chunk, s, length, qkv, kv, mask_ref, cot_ref, out_ref, bias, put_grad):
    scale = HEAD ** (-0.5)
    ctx = kv.shape[2] - TREE
    heads = cot_ref.shape[1] // HEAD
    here = _at(s * TREE, TREE)
    cols = lax.broadcasted_iota(jnp.int32, (TREE, ctx), 1)
    bias[:, :ctx] = jnp.where(cols < length, 0.0, -1e30)
    bias[:, ctx:] = jnp.where(mask_ref[s] == 1, 0.0, -1e30)
    dkey = jnp.zeros((HEAD, TREE), F32)
    dvalue = jnp.zeros((HEAD, TREE), F32)
    for first in range(0, heads, chunk):
        def rows(ref):
            return jnp.concatenate(
                [ref[here, h * HEAD:(h + 1) * HEAD] for h in range(first, first + chunk)], axis=0)
        q = rows(qkv)
        cot = rows(cot_ref)
        score = _dot(q, kv[0, s], ((1,), (1,))) * scale
        score = (score.reshape(chunk, TREE, -1) + bias[...][None]).reshape(chunk * TREE, -1)
        e = jnp.exp(score - jnp.max(score, axis=1, keepdims=True))
        probs = e * (1.0 / jnp.sum(e, axis=1, keepdims=True))
        low = probs.astype(BF16)
        dprob = _dot(cot, kv[1, s], ((1,), (1,)))
        delta = jnp.sum(probs * dprob, axis=1, keepdims=True)
        dscore = ((probs * scale) * (dprob - delta)).astype(BF16)
        out = _dot(low, kv[1, s], ((1,), (0,))).astype(BF16)
        dq = _dot(dscore, kv[0, s], ((1,), (0,)))
        for k in range(chunk):
            h = first + k
            out_ref[here, h * HEAD:(h + 1) * HEAD] = out[k * TREE:(k + 1) * TREE]
            put_grad(h, dq[k * TREE:(k + 1) * TREE].T.astype(BF16))
        dkey += _dot(q, dscore[:, ctx:], ((0,), (0,)))
        dvalue += _dot(cot, low[:, ctx:], ((0,), (0,)))
    put_grad(heads, dkey.astype(BF16))
    put_grad(heads + 1, dvalue.astype(BF16))


def train_kernel(order_ref, len_ref, parent_ref, feat_hbm, mask_hbm, cot_hbm, ctx_ref, wq_ref, wk_ref, wv_ref,
                 out_ref, gq_ref, gk_ref, gv_ref,
                 feat_ref, mask_ref, cot_ref, spread, staged, kv, flat, weight, acc, qkv, bias,
                 group_flat, group_grad, term, arrived, far, far_in, own, across, landed,
                 ctx_send, ctx_recv, slot_send, slot_recv, mp_send, mp_recv, weight_sem,
                 early_send, early_recv, late_send, late_recv, pass_send, pass_recv, grad_send, grad_recv, relay_send, relay_recv, term_send, term_recv, far_send, far_recv,
                 y_send, y_recv, copy_sem, in_sem, plane_in, all_in):
    axes = ("x", "z")
    n = lax.axis_size("x")
    n_y = lax.axis_size("y_hi")
    wide = n_y * n * n
    slots = mask_ref.shape[0]
    rows = slots * TREE
    width = flat.shape[4]
    part = spread.shape[2]
    half_cols = group_grad.shape[1]
    blocks = half_cols // HEAD
    core = lax.axis_index("core")
    y_lo = lax.axis_index("y_lo")
    here = [lax.axis_index(a) for a in axes]
    y_me = lax.axis_index("y_hi")
    me = (y_me * n + here[1]) * n + here[0]

    steps = [(a, b, c) for a in range(n_y) for b in range(n) for c in range(n)]
    ring = [[lax.rem(here[k] + d, n) for d in range(n)] for k in range(2)]
    y_ring = [y_me, 1 - y_me]
    index = [(y_ring[a] * n + ring[1][b]) * n + ring[0][c] for a, b, c in steps]
    trainer = [{"y_hi": y_ring[a], "z": ring[1][b], "x": ring[0][c]} for a, b, c in steps]

    plane = n * n
    in_row, in_column = range(1, n), range(n, plane, n)
    loads = [pltpu.make_async_copy(src, dst, in_sem.at[k]) for k, (src, dst) in enumerate(
        ((feat_hbm, feat_ref), (mask_hbm, mask_ref), (cot_hbm, cot_ref)))]
    for c in loads:
        c.start()
    barrier = pltpu.get_barrier_semaphore()
    for axis in MP:
        pl.semaphore_signal(barrier, inc=1, device_id=_peer(axis, 1), device_id_type=MESH)
    for d in (plane, *in_row, *in_column):
        pl.semaphore_signal(barrier, inc=1, device_id=trainer[d], device_id_type=MESH)

    def shard(a, c, s):
        return flat.at[a, pl.ds(c * 2, 2), :, s * TREE:(s + 1) * TREE]

    def mp_copy(k, s):
        a = (y_lo, y_lo, 1 - y_lo)[k]
        return pltpu.make_async_remote_copy(
            src_ref=shard(a, core, s), dst_ref=shard(a, core, s), send_sem=mp_send.at[k, s], recv_sem=mp_recv.at[k, s],
            device_id=_peer("y_lo" if k == 0 else "core", 1), device_id_type=MESH)

    loads[0].wait()
    for s in range(slots):
        node = lax.broadcasted_iota(jnp.int32, (TREE, TREE), 0)
        same = node == lax.broadcasted_iota(jnp.int32, (TREE, TREE), 1)
        pick = (node == parent_ref[s:s + 1, :]).astype(F32) + same.astype(F32)
        mixed = _dot(pick.astype(BF16), feat_ref[s], ((0,), (0,))).astype(BF16)
        for k in range(2):
            for x in range(n):
                at = (k * n + x) * width
                flat[y_lo, 2 * core + k, x, s * TREE:(s + 1) * TREE, :] = mixed[:, at:at + width]
    pl.semaphore_wait(barrier, 2 * n + 1)
    for d in in_column:
        pl.semaphore_signal(plane_in, inc=1, device_id=trainer[d], device_id_type=MESH)

    def spread_copy(d):
        return pltpu.make_async_remote_copy(
            src_ref=ctx_ref.at[:, :, _at(index[d] * part, part)], dst_ref=spread.at[:, pl.ds(me * slots, slots)],
            send_sem=ctx_send.at[d], recv_sem=ctx_recv.at[d], device_id=trainer[d], device_id_type=MESH)

    def plane_copy(d):
        return pltpu.make_async_remote_copy(
            src_ref=staged.at[:, pl.ds(index[d] * slots, slots)], dst_ref=kv.at[:, :, _at(me * part, part)],
            send_sem=slot_send.at[slots, d], recv_sem=slot_recv.at[slots, d],
            device_id=trainer[d], device_id_type=MESH)

    def cross_copy(s, d):
        return pltpu.make_async_remote_copy(
            src_ref=staged.at[:, index[d] * slots + s], dst_ref=kv.at[:, s, _at(me * part, part)],
            send_sem=slot_send.at[s, d - plane], recv_sem=slot_recv.at[s, d - plane],
            device_id=trainer[d], device_id_type=MESH)

    def start_cross(s):
        for d in range(plane, wide):
            cross_copy(s, d).start()

    own_ctx = pltpu.make_async_copy(
        ctx_ref.at[:, :, _at(me * part, part)], spread.at[:, pl.ds(me * slots, slots)], ctx_recv.at[0])
    for k in range(2):
        for s in range(1 if k == 0 else slots):
            mp_copy(k, s).start()
    for d in (plane, *in_row, *in_column):
        spread_copy(d).start()
    own_ctx.start()
    pl.semaphore_wait(plane_in, n - 1)
    pl.semaphore_signal(all_in, inc=1, device_id=trainer[plane], device_id_type=MESH)
    for d in range(1, plane):
        if d not in in_row and d not in in_column:
            spread_copy(d).start()
    pl.semaphore_wait(all_in, 1)
    for d in range(plane + 1, wide):
        spread_copy(d).start()

    depth = weight.shape[1]
    buffers = weight.shape[0]
    sources = [(y_lo, core), (y_lo, 1 - core), (1 - y_lo, core), (1 - y_lo, 1 - core)]
    chunks = [(a, 2 * c + k) for a, c in sources for k in range(2)]

    def weight_copies(i):
        a, z = chunks[i]
        at = _at((a * n + z) * depth, depth)
        slot = i % buffers
        q_cols, kv_cols = wq_ref.shape[1], wk_ref.shape[1]
        return [
            pltpu.make_async_copy(wq_ref.at[at], weight.at[slot, :, :q_cols], weight_sem.at[slot, 0]),
            pltpu.make_async_copy(wk_ref.at[at], weight.at[slot, :, q_cols:q_cols + kv_cols], weight_sem.at[slot, 1]),
            pltpu.make_async_copy(wv_ref.at[at], weight.at[slot, :, q_cols + kv_cols:], weight_sem.at[slot, 2]),
        ]

    for i in range(buffers):
        for c in weight_copies(i):
            c.start()

    def early_copy(half, d):
        to = _peer(axes[half], d)
        at = to[axes[half]]
        mine = pl.ds(core * 2, 2)
        return pltpu.make_async_remote_copy(
            src_ref=flat.at[y_lo, mine, at] if half == 0 else flat.at[y_lo, at, mine],
            dst_ref=group_flat.at[half, y_lo, mine, _at(here[half] * rows, rows)],
            send_sem=early_send.at[half, d - 1], recv_sem=early_recv.at[half, d - 1],
            device_id=to, device_id_type=MESH)

    def late_copy(half, s, d):
        to = _peer(axes[half], d)
        at = to[axes[half]]
        mine = pl.ds(core * 2, 2)
        src_rows = pl.ds(s * TREE, TREE)
        return pltpu.make_async_remote_copy(
            src_ref=flat.at[1 - y_lo, mine, at, src_rows] if half == 0 else flat.at[1 - y_lo, at, mine, src_rows],
            dst_ref=group_flat.at[half, 1 - y_lo, mine, _at((here[half] * slots + s) * TREE, TREE)],
            send_sem=late_send.at[half, s, d - 1], recv_sem=late_recv.at[half, s, d - 1],
            device_id=to, device_id_type=MESH)

    def pass_copy(late, half, d):
        a = 1 - y_lo if late else y_lo
        ref = group_flat.at[half, a, pl.ds(core * 2, 2), _at(ring[half][n - d] * rows, rows)]
        return pltpu.make_async_remote_copy(
            src_ref=ref, dst_ref=ref, send_sem=pass_send.at[late, half, d - 1], recv_sem=pass_recv.at[late, half, d - 1],
            device_id=_peer("core", 1), device_id_type=MESH)

    def own_copy(half, y):
        src = flat.at[y, :, here[half]] if half == 0 else flat.at[y, here[half]]
        return pltpu.make_async_copy(src, group_flat.at[half, y, :, _at(here[half] * rows, rows)], copy_sem.at[half, y])

    def grad_copy(half, s, d):
        ref = group_grad.at[half, :, _at((here[half] * slots + s) * TREE, TREE)]
        return pltpu.make_async_remote_copy(
            src_ref=ref, dst_ref=ref, send_sem=grad_send.at[half, s, d // 2], recv_sem=grad_recv.at[half, s, d // 2],
            device_id=_peer(axes[half], d), device_id_type=MESH)

    def relay_copy(half, s, d):
        member = ring[half][n - d]
        mid = half_cols // 2
        ref = group_grad.at[half, pl.ds(0 if d == 1 else mid, mid), _at((member * slots + s) * TREE, TREE)]
        return pltpu.make_async_remote_copy(
            src_ref=ref, dst_ref=ref, send_sem=relay_send.at[half, s, d // 2], recv_sem=relay_recv.at[half, s, d // 2],
            device_id=_peer(axes[half], d), device_id_type=MESH)

    near = [(half, d) for half in range(2) for d in (1, n - 1)]

    def relay(s):
        for half, d in near:
            grad_copy(half, s, d).wait_recv()
            relay_copy(half, s, d).start()

    split = (blocks + 1) // 2 * HEAD
    parts = [(0, split), (split, half_cols)]

    def term_copy(p, half, d):
        cols = pl.ds(parts[p][0], parts[p][1] - parts[p][0])
        return pltpu.make_async_remote_copy(
            src_ref=term.at[half, d // 2, :, cols], dst_ref=arrived.at[half, d // 2, :, cols],
            send_sem=term_send.at[p, half, d // 2], recv_sem=term_recv.at[p, half, d // 2],
            device_id=_peer(axes[1 - half], d), device_id_type=MESH)

    def far_copy(p, half, y):
        cols = pl.ds(parts[p][0], parts[p][1] - parts[p][0])
        return pltpu.make_async_remote_copy(
            src_ref=far.at[half, y, cols], dst_ref=far_in.at[half, y, cols],
            send_sem=far_send.at[p, half, y], recv_sem=far_recv.at[p, half, y],
            device_id=_peer(axes[1 - half], (1, n - 1)[y]), device_id_type=MESH)

    def y_copy(p, half):
        cols = pl.ds(parts[p][0], parts[p][1] - parts[p][0])
        return pltpu.make_async_remote_copy(
            src_ref=across.at[half, cols], dst_ref=landed.at[half, cols],
            send_sem=y_send.at[p, half], recv_sem=y_recv.at[p, half],
            device_id=_peer("y_hi", 1), device_id_type=MESH)

    both = [(half, d) for d in range(1, n) for half in range(2)]


    def project(i):
        a, z = chunks[i]
        for c in weight_copies(i):
            c.wait()
        lhs = jnp.concatenate([flat[a, z, x] for x in range(n)], axis=1)
        product = _dot(lhs, weight[i % buffers], ((1,), (0,)))
        if i == 0:
            acc[...] = product
        else:
            acc[...] += product
        if i + buffers < len(chunks):
            for c in weight_copies(i + buffers):
                c.start()

    for d in range(1, n):
        early_copy(0, d).start()
    project(0)
    project(1)
    for s in range(slots):
        mp_copy(1, s).wait_recv()
    for d in range(1, n):
        early_copy(1, d).start()
    mp_copy(0, 1).start()
    project(2)
    project(3)

    for d in range(1, wide):
        spread_copy(d).wait_recv()
    own_ctx.wait()
    for s in range(2, slots):
        mp_copy(0, s).start()

    def place(r, carry):
        staged[:, r] = spread[:, order_ref[r]]
        return carry

    lax.fori_loop(0, wide * slots, place, 0, unroll=8)
    for d in range(1, plane):
        plane_copy(d).start()
    own_slots = pltpu.make_async_copy(
        staged.at[:, pl.ds(me * slots, slots)], kv.at[:, :, _at(me * part, part)], copy_sem.at[2, 0])
    own_slots.start()

    def sibling_arrived(s):
        mp_copy(2, s).wait_recv()
        for d in range(1, n):
            late_copy(1, s, d).start()

    for s in range(slots):
        mp_copy(0, s).wait_recv()
        mp_copy(2, s).start()
        for d in range(1, n):
            late_copy(0, s, d).start()
        if s > 0:
            start_cross(s - 1)
            sibling_arrived(s - 1)
        if s == slots - 1:
            for half, d in both:
                early_copy(half, d).wait_recv()
                pass_copy(0, half, d).start()
    project(4)
    project(5)
    start_cross(slots - 1)
    sibling_arrived(slots - 1)
    for half in range(2):
        for y in range(2):
            own_copy(half, y).start()
    project(6)
    project(7)
    ctx_len = kv.shape[2] - TREE
    q_cols = wq_ref.shape[1]
    qkv[...] = acc[:, :q_cols].astype(BF16)
    for s in range(slots):
        for k in range(2):
            kv[k, s, ctx_len:] = acc[s * TREE:(s + 1) * TREE, q_cols + k * HEAD:q_cols + (k + 1) * HEAD].astype(BF16)
    for c in loads[1:]:
        c.wait()
    own_slots.wait()
    for d in range(1, plane):
        plane_copy(d).wait_recv()

    def slot_step(s, carry):
        def put_grad(column, block):
            half, at = divmod(column, blocks)
            group_grad[half, at * HEAD:(at + 1) * HEAD, _at((here[half] * slots + s) * TREE, TREE)] = block
        @pl.when(s == slots - 1)
        def _():
            for half, d in both:
                for k in range(slots):
                    late_copy(half, k, d).wait_recv()
                pass_copy(1, half, d).start()
        for d in range(plane, wide):
            cross_copy(s, d).wait_recv()
        attend_slot(2, s, len_ref[order_ref[me * slots + s]], qkv, kv, mask_ref, cot_ref, out_ref, bias, put_grad)
        for half, d in near:
            grad_copy(half, s, d).start()

        @pl.when(s > 0)
        def _():
            relay(s - 1)
        return carry

    lax.fori_loop(0, slots, slot_step, 0)
    relay(slots - 1)

    for half in range(2):
        for y in range(2):
            own_copy(half, y).wait()
    for late in range(2):
        for half, d in both:
            pass_copy(late, half, d).wait_recv()
    for s in range(slots):
        for half, d in near:
            relay_copy(half, s, d).wait_recv()

    def product(p, half, d, y):
        lo, hi = parts[p]
        return _dot(group_grad[half, lo:hi], group_flat[half, y, ring[1 - half][d]], ((1,), (0,)))

    for p, (lo, hi) in enumerate(parts):
        for half in range(2):
            for y in range(n_y):
                far[half, y, lo:hi] = product(p, half, 2, y).astype(BF16)
                far_copy(p, half, y).start()
    for p, (lo, hi) in enumerate(parts):
        for half in range(2):
            for y in range(n_y):
                own[half, y, lo:hi] = product(p, half, 0, y)
        for half, d in near:
            y = d // 2
            term[half, d // 2, 1 - y, lo:hi] = product(p, half, d, 1 - y).astype(BF16)
            far_copy(p, half, y).wait_recv()
            term[half, d // 2, y, lo:hi] = (product(p, half, d, y) + far_in[half, y, lo:hi].astype(F32)).astype(BF16)
            term_copy(p, half, d).start()

    def total(p, half, y):
        lo, hi = parts[p]
        out = own[half, y, lo:hi]
        for k in range(2):
            out += arrived[half, k, y, lo:hi].astype(F32)
        return out

    for p, (lo, hi) in enumerate(parts):
        for half in range(2):
            for d in (1, n - 1):
                term_copy(p, half, d).wait_recv()
            across[half, lo:hi] = total(p, half, 1 - y_me).astype(BF16)
            y_copy(p, half).start()
        for half in range(2):
            own[half, y_me, lo:hi] = total(p, half, y_me)
    for p, (lo, hi) in enumerate(parts):
        for half in range(2):
            y_copy(p, half).wait_recv()
            final = (own[half, y_me, lo:hi] + landed[half, lo:hi].astype(F32)).T
            for k in range(lo // HEAD, hi // HEAD):
                h = half * blocks + k
                ref, at = (gq_ref, h) if h < q_cols // HEAD else ((gk_ref, gv_ref)[h - q_cols // HEAD], 0)
                ref[:, at * HEAD:(at + 1) * HEAD] = final[:, k * HEAD - lo:(k + 1) * HEAD - lo]

    for half, d in both:
        early_copy(half, d).wait_send()
        for k in range(2):
            pass_copy(k, half, d).wait_send()
        for s in range(slots):
            late_copy(half, s, d).wait_send()
    for half, d in near:
        for p in range(2):
            term_copy(p, half, d).wait_send()
            far_copy(p, half, d // 2).wait_send()
        for s in range(slots):
            grad_copy(half, s, d).wait_send()
            relay_copy(half, s, d).wait_send()
    for p in range(2):
        for half in range(2):
            y_copy(p, half).wait_send()
    for k in range(3):
        for s in range(slots):
            mp_copy(k, s).wait_send()
    for d in range(1, wide):
        spread_copy(d).wait_send()
    for d in range(1, plane):
        plane_copy(d).wait_send()
    for s in range(slots):
        for d in range(plane, wide):
            cross_copy(s, d).wait_send()


def hand_on_kernel(*refs):
    n = len(refs) // 2
    for k in range(n):
        refs[n + k][...] = refs[k][...]


def hand_on(arrays):
    vmem = pl.BlockSpec(memory_space=pltpu.VMEM)
    return pl.pallas_call(
        hand_on_kernel,
        in_specs=[vmem] * len(arrays),
        out_specs=[vmem] * len(arrays),
        out_shape=[jax.ShapeDtypeStruct(a.shape, a.dtype) for a in arrays],
    )(*arrays)


def local(
    context_kv,
    train_order,
    prompt_lengths,
    parent_nodes,
    tree_mask,
    tree_features,
    query_weight,
    key_weight,
    value_weight,
    cotangent,
):
    slots, _, feat_cols = tree_features.shape
    rows = slots * TREE
    n_y, n, _ = [lax.axis_size(a) for a in WIDE]
    wide = n_y * n * n
    ctx = context_kv.shape[2]
    part = ctx // wide
    width = query_weight.shape[0] // wide
    q_cols = query_weight.shape[1]
    kv_cols = key_weight.shape[1]
    cols = q_cols + 2 * kv_cols
    half_cols = cols // 2
    smem = pl.BlockSpec(memory_space=pltpu.SMEM)
    vmem = pl.BlockSpec(memory_space=pltpu.VMEM)
    hbm = pl.BlockSpec(memory_space=pl.ANY)
    dma = pltpu.SemaphoreType.DMA
    results = pl.pallas_call(
        train_kernel,
        in_specs=[smem, smem, vmem] + [hbm] * 7,
        out_specs=[vmem] * 4,
        out_shape=[
            jax.ShapeDtypeStruct((rows, q_cols), BF16),
            jax.ShapeDtypeStruct((width, q_cols), F32),
            jax.ShapeDtypeStruct((width, kv_cols), F32),
            jax.ShapeDtypeStruct((width, kv_cols), F32),
        ],
        scratch_shapes=[
            pltpu.VMEM(tree_features.shape, BF16),
            pltpu.VMEM(tree_mask.shape, jnp.int32),
            pltpu.VMEM((rows, q_cols), BF16),
            pltpu.VMEM((2, wide * slots, part, HEAD), BF16),
            pltpu.VMEM((2, wide * slots, part, HEAD), BF16),
            pltpu.VMEM((2, slots, ctx + TREE, HEAD), BF16),
            pltpu.VMEM((n_y, n, n, rows, width), BF16),
            pltpu.VMEM((3, n * width, cols), BF16),
            pltpu.VMEM((rows, cols), F32),
            pltpu.VMEM((rows, q_cols), BF16),
            pltpu.VMEM((TREE, ctx + TREE), F32),
            pltpu.VMEM((2, n_y, n, n * rows, width), BF16),
            pltpu.VMEM((2, half_cols, n * rows), BF16),
            pltpu.VMEM((2, 2, n_y, half_cols, width), BF16),
            pltpu.VMEM((2, 2, n_y, half_cols, width), BF16),
            pltpu.VMEM((2, n_y, half_cols, width), BF16),
            pltpu.VMEM((2, n_y, half_cols, width), BF16),
            pltpu.VMEM((2, n_y, half_cols, width), F32),
            pltpu.VMEM((2, half_cols, width), BF16),
            pltpu.VMEM((2, half_cols, width), BF16),
            dma((wide,)), dma((wide,)), dma((slots + 1, n * n)), dma((slots + 1, n * n)),
            dma((3, slots)), dma((3, slots)), dma((3, 3)),
            dma((2, n - 1)), dma((2, n - 1)), dma((2, slots, n - 1)), dma((2, slots, n - 1)),
            dma((2, 2, n - 1)), dma((2, 2, n - 1)),
            dma((2, slots, 2)), dma((2, slots, 2)), dma((2, slots, 2)), dma((2, slots, 2)),
            dma((2, 2, 2)), dma((2, 2, 2)), dma((2, 2, 2)), dma((2, 2, 2)),
            dma((2, 2)), dma((2, 2)), dma((3, 2)), dma((3,)), pltpu.SemaphoreType.REGULAR, pltpu.SemaphoreType.REGULAR,
        ],
        compiler_params=pltpu.CompilerParams(
            collective_id=0, has_side_effects=True, vmem_limit_bytes=63 * 1024 * 1024),
    )(train_order, prompt_lengths, parent_nodes, tree_features, tree_mask, cotangent.reshape(rows, q_cols),
      context_kv, query_weight, key_weight, value_weight)
    attended, query_gradient, key_gradient, value_gradient = hand_on(results)
    return (attended.reshape(slots, TREE, q_cols), query_gradient, key_gradient, value_gradient)


def solution(mesh):
    cube = Mesh(mesh.devices.reshape(2, 4, 4, 2, 2), WIDE + MP)
    return jax.shard_map(
        local,
        mesh=cube,
        in_specs=(
            P(None, WIDE, None, MP),
            P(),
            P(),
            P(WIDE, None),
            P(WIDE, None, None),
            P(WIDE, None, MP),
            P(None, MP),
            P(None, MP),
            P(None, MP),
            P(WIDE, None, MP),
        ),
        out_specs=(P(WIDE, None, MP), P(WIDE, MP), P(WIDE, MP), P(WIDE, MP)),
        check_vma=False,
    )
```
